256 devices in a mesh: row: 16 (over x, z_lo), col: 16 (over z_hi, y, core).
Axes of the slice: x: 4, y: 4, z: 8 (z_hi: 2, z_lo: 4; z = z_hi * 4 + z_lo), core: 2. Of those that a mesh axis runs over, the one named last changes fastest.
Arguments:
- features_in: bfloat16 [256, 2048, 256], P('row', 'col'), may hold values from -6 to 6
- stencil: bfloat16 [3, 7, 256, 2048], P(None, None, 'row', 'col'), may hold values from -2.5 to 2.5
- weights_first: bfloat16 [4, 256, 256], replicated, may hold values from -0.1875 to 0.1875
- weights_second: bfloat16 [4, 256, 256], replicated, may hold values from -0.1875 to 0.1875
- cotangent: bfloat16 [256, 2048, 256], P('row', 'col'), may hold values from -6 to 6
Outputs:
- input_grad: bfloat16 [256, 2048, 256], P('row', 'col')
- grad_first: float32 [4, 256, 256], replicated
- grad_second: float32 [4, 256, 256], replicated
The draws below stay inside these ranges and needn't reach their ends.
All inputs are finite; a program needn't handle non-finite values.
Results may differ from the reference program's by a relative error of at most 0.0068.
Values may be sent and summed in bfloat16 or wider, within the bound.
No kernel may reach another device: no remote copies, remote signals or barrier semaphores. Data moves between devices by JAX's collectives and lax.ppermute only.
A program may use at most 128 MiB of HBM per device.

```python
import math
import jax
import jax.numpy as jnp
from jax import lax

C = 256
NR = 256
NC = 2048


def block_levels(rng, shape, shards, low, high):
    loudness = 1.0
    for dim, parts in shards:
        heights = jax.random.uniform(jax.random.fold_in(jax.random.fold_in(rng, 6), dim), (parts,), jnp.float32, low / len(shards), high / len(shards))
        loudness = loudness * jnp.repeat(jnp.exp(heights), shape[dim] // parts).reshape((-1,) + (1,) * (len(shape) - 1 - dim))
    return loudness


def gaussian(stream_key, extent, deviation, limit, shards=(), held_as=jnp.bfloat16):
    values = deviation * jax.random.normal(stream_key, extent, jnp.float32)
    if shards:
        values = values * block_levels(stream_key, extent, shards, -0.22, 0.18)
    return jnp.clip(values, -limit, limit).astype(held_as)


def setup_inputs(seed: int = 0) -> dict:
    arg_keys = jax.random.split(jax.random.key(seed), 6)
    features_in = gaussian(arg_keys[0], (NR, NC, C), 1.0, 6.0, ((0, 16), (1, 16)))
    stencil = gaussian(arg_keys[1], (3, 7, NR, NC), 0.4, 2.5, ((2, 16), (3, 16)))
    weights_first = gaussian(arg_keys[2], (4, C, C), (4 * C) ** -0.5, 0.1875)
    weights_second = gaussian(arg_keys[3], (4, C, C), (4 * C) ** -0.5, 0.1875)
    cotangent = gaussian(arg_keys[4], (NR, NC, C), 1.0, 6.0, ((0, 16), (1, 16)))
    return dict(features_in=features_in, stencil=stencil, weights_first=weights_first, weights_second=weights_second, cotangent=cotangent)


OFFSETS = ((0, 0), (0, 1), (0, -1), (1, 0), (-1, 0), (1, 1), (-1, -1))

def extend(field, row_axis):
    col_axis = row_axis + 1
    widths = [(0, 0)] * field.ndim
    widths[row_axis] = (1, 1)
    taller = jnp.pad(field, widths)
    length = taller.shape[col_axis]
    leading = lax.slice_in_dim(taller, 0, 1, axis=col_axis)
    trailing = lax.slice_in_dim(taller, length - 1, length, axis=col_axis)
    return jnp.concatenate([trailing, taller, leading], axis=col_axis)

def stencil_apply(extended, coefficient, height, breadth):
    accumulated = None
    for position, (row_step, col_step) in enumerate(OFFSETS):
        portion = extended[1 + row_step:1 + row_step + height, 1 + col_step:1 + col_step + breadth]
        addend = coefficient[position][:, :, None] * portion.astype(jnp.float32)
        accumulated = addend if position == 0 else accumulated + addend
    return accumulated

def feature_stack(field, coefficients):
    height, breadth = (field.shape[0], field.shape[1])
    extended = extend(field, 0)
    stacked = [field]
    for operator in range(3):
        stacked.append(stencil_apply(extended, coefficients[operator], height, breadth).astype(jnp.bfloat16))
    return jnp.concatenate(stacked, axis=2)

def transposed(directional, extended_weights, channels):
    height, breadth = (directional.shape[0], directional.shape[1])
    extended = extend(directional, 0)
    accumulated = None
    for operator in range(3):
        for position, (row_step, col_step) in enumerate(OFFSETS):
            row_start = 1 - row_step
            col_start = 1 - col_step
            weight_part = extended_weights[operator, position, row_start:row_start + height, col_start:col_start + breadth]
            field_part = extended[row_start:row_start + height, col_start:col_start + breadth, operator * channels:(operator + 1) * channels]
            addend = weight_part[:, :, None] * field_part.astype(jnp.float32)
            accumulated = addend if accumulated is None else accumulated + addend
    return accumulated

def backward_input(grad_flat, weights, extended_weights, height, breadth, channels):
    projected = jnp.dot(grad_flat, weights.reshape(-1, channels).T, preferred_element_type=jnp.float32).astype(jnp.bfloat16)
    centre = projected[:, :channels].astype(jnp.float32)
    directional = projected[:, channels:].reshape(height, breadth, 3 * channels)
    return centre + transposed(directional, extended_weights, channels).reshape(-1, channels)

def reference(features_in, stencil, weights_first, weights_second, cotangent):
    height, breadth, channels = features_in.shape
    coefficients = stencil.astype(jnp.float32)
    extended_weights = extend(coefficients, 2)
    scale_factor = 1.0 / math.sqrt(NR * NC)
    first_stack = feature_stack(features_in, coefficients)
    first_flat = first_stack.reshape(-1, 4 * channels)
    first_pre = jnp.dot(first_flat, weights_first.reshape(-1, channels), preferred_element_type=jnp.float32)
    hidden = jax.nn.silu(first_pre).astype(jnp.bfloat16).reshape(height, breadth, channels)
    second_flat = feature_stack(hidden, coefficients).reshape(-1, 4 * channels)
    cot_flat = cotangent.reshape(-1, channels)
    grad_second = (jnp.dot(second_flat.T, cot_flat, preferred_element_type=jnp.float32) * scale_factor).reshape(4, channels, channels)
    hidden_grad = backward_input(cot_flat, weights_second, extended_weights, height, breadth, channels)
    sigmoid_value = jax.nn.sigmoid(first_pre)
    pre_grad = (hidden_grad * sigmoid_value * (1.0 + first_pre * (1.0 - sigmoid_value))).astype(jnp.bfloat16)
    grad_first = (jnp.dot(first_flat.T, pre_grad, preferred_element_type=jnp.float32) * scale_factor).reshape(4, channels, channels)
    input_grad = backward_input(pre_grad, weights_first, extended_weights, height, breadth, channels)
    input_grad = input_grad.astype(jnp.bfloat16).reshape(height, breadth, channels)
    return (input_grad, grad_first, grad_second)
```

```python
import functools
import math

import jax
import jax.numpy as jnp
from jax import lax
from jax.experimental import pallas as pl
from jax.experimental.pallas import tpu as pltpu
from jax.sharding import PartitionSpec as P

F32 = jnp.float32
BF16 = jnp.bfloat16
BOTH = ("row", "col")
SLOTS = 32
VMEM_LIMIT = 56 * 1024 * 1024


def dot(lhs, rhs, lhs_dim, rhs_dim):
    return lax.dot_general(
        lhs, rhs, (((lhs_dim,), (rhs_dim,)), ((), ())), preferred_element_type=F32
    )


def iota(shape, dim):
    return lax.broadcasted_iota(jnp.int32, shape, dim)


def as_mask(condition):
    return jnp.where(condition, 1.0, 0.0).astype(BF16)


def halves(value):
    return jnp.concatenate([value[:, :128], value[:, 128:]], axis=0)


def whole(ref, start, rows):
    return jnp.concatenate([ref[start : start + rows], ref[start + rows : start + 2 * rows]], axis=1)


def pack_kernel(f_ref, c_ref, st_ref, stt_ref, up_ref, down_ref, left_ref, right_ref, ul_ref, dr_ref):
    height, breadth, _ = f_ref.shape
    for row, out in ((0, up_ref), (height - 1, down_ref)):
        out[0 : 2 * breadth] = halves(f_ref[row])
        out[2 * breadth : 4 * breadth] = halves(c_ref[row])
        out[4 * breadth : 4 * breadth + SLOTS] = stt_ref[row]
    for col, first, out in ((0, (2, 6), left_ref), (breadth - 1, (1, 5), right_ref)):
        base = 0 if col == 0 else breadth - 16
        for which, ref in enumerate((f_ref, c_ref)):
            edge = ref[:, base : base + 16, :].astype(F32)[:, col - base, :]
            out[which * 2 * height : (which + 1) * 2 * height] = halves(edge).astype(BF16)
        for which, slot in enumerate(first):
            for k in range(3):
                start = 4 * height + (which * 3 + k) * height
                out[start : start + height] = st_ref[7 * k + slot]
    for row, col, slot, out in ((0, 0, 6, ul_ref), (height - 1, breadth - 1, 5, dr_ref)):
        base = 0 if col == 0 else breadth - 16
        lines = []
        for ref in (f_ref, c_ref):
            edge = ref[row, base : base + 16, :].astype(F32)[col - base : col - base + 1]
            lines += [edge[:, :128], edge[:, 128:]]
        weights = stt_ref[row].astype(F32)
        lines += [weights[7 * k + slot : 7 * k + slot + 1] for k in range(3)]
        lines.append(jnp.zeros((16 - len(lines), 128), F32))
        out[...] = jnp.concatenate(lines, axis=0).astype(BF16)


def pack(features, cotangent, stencil, stencil_t):
    height, breadth, _ = features.shape
    sizes = (4 * breadth + SLOTS,) * 2 + (10 * height,) * 2 + (16, 16)
    return pl.pallas_call(
        pack_kernel,
        out_shape=[jax.ShapeDtypeStruct((n, 128), BF16) for n in sizes],
        compiler_params=pltpu.CompilerParams(vmem_limit_bytes=VMEM_LIMIT),
        name="pack_rims",
    )(features, cotangent, stencil, stencil_t)


def exchange(messages, joint):
    up, down, left, right, up_left, down_right = messages
    rows, cols = lax.axis_size("row"), lax.axis_size("col")
    index = lambda r, c: r * cols + c % cols
    below = lax.ppermute(up, "row", [(i + 1, i) for i in range(rows - 1)])
    above = lax.ppermute(down, "row", [(i, i + 1) for i in range(rows - 1)])
    right_rim = lax.ppermute(left, "col", [((i + 1) % cols, i) for i in range(cols)])
    left_rim = lax.ppermute(right, "col", [(i, (i + 1) % cols) for i in range(cols)])
    corner_br = lax.ppermute(
        up_left, BOTH, [(index(r + 1, c + 1), index(r, c)) for r in range(rows - 1) for c in range(cols)]
    )
    corner_tl = lax.ppermute(
        down_right, BOTH, [(index(r, c), index(r + 1, c + 1)) for r in range(rows - 1) for c in range(cols)]
    )
    return above, below, left_rim, right_rim, corner_tl, corner_br


def fill_masks(mask_ref):
    j, c = iota((128, 128), 0), iota((128, 128), 1)
    mask_ref[0] = as_mask(j == c)
    mask_ref[1] = as_mask(j == c + 1)
    mask_ref[2] = as_mask(j == c - 1)
    mask_ref[3] = as_mask(((j == 0) & (c < 2)) | ((j == 127) & ((c == 2) | (c == 3))))
    e, l = iota((16, 128), 0), iota((16, 128), 1)
    spots = ((0, 0), (1, 0), (2, 127), (3, 127))
    for number, (edge, lane) in enumerate(spots):
        mask_ref[4, 16 * number : 16 * number + 16] = as_mask((e == edge) & (l == lane))


def fill_weights(stt_ref, above_ref, below_ref, left_ref, right_ref, tl_ref, br_ref, wx_ref, we_ref):
    height, _, breadth = stt_ref.shape
    base = 4 * breadth
    wx_ref[0] = above_ref[base : base + SLOTS].astype(F32)
    for r in range(height):
        wx_ref[1 + r] = stt_ref[r].astype(F32)
    wx_ref[height + 1] = below_ref[base : base + SLOTS].astype(F32)
    lane = iota((height, 128), 1)

    def spot(value, shift, place):
        rolled = pltpu.roll(value.astype(F32), shift, 1)
        return jnp.where(lane[: value.shape[0]] == place, rolled, 0.0)

    for k in range(3):
        near = 4 * height + k * height
        far = near + 3 * height
        we_ref[0, k, 8 : 8 + height] = spot(left_ref[near : near + height], 1, 0) + spot(
            right_ref[near : near + height], 2, 2
        )
        we_ref[1, k, 8 : 8 + height] = spot(left_ref[far : far + height], 2, 1)
        we_ref[1, k, 0:8] = jnp.broadcast_to(spot(tl_ref[...], 2, 1)[4 + k : 5 + k], (8, 128))
        we_ref[2, k, 8 : 8 + height] = spot(right_ref[far : far + height], 3, 3)
        we_ref[2, k, 8 + height : 16 + height] = jnp.broadcast_to(
            spot(br_ref[...], 3, 3)[4 + k : 5 + k], (8, 128)
        )


def fill_sides(left, right, tl, br, lx_ref, rx_ref):
    height = left.shape[0]
    lx_ref[0:8] = jnp.broadcast_to(tl.astype(F32), (8, tl.shape[1]))
    lx_ref[8 : 8 + height] = left.astype(F32)
    rx_ref[0:height] = right.astype(F32)
    rx_ref[height : height + 8] = jnp.broadcast_to(br.astype(F32), (8, br.shape[1]))


def line(weights, slot):
    return jnp.broadcast_to(weights[slot : slot + 1], (16, 128)).astype(BF16)


def tall(value):
    return jnp.concatenate([value] * 8, axis=0)


def field_block(ext_ref, lx_ref, rx_ref, r):
    channels = ext_ref.shape[2]
    e = iota((16, channels), 0)
    edge = jnp.where(e == 0, lx_ref[pl.ds(r + 8, 1)], 0.0)
    edge = jnp.where(e == 1, lx_ref[pl.ds(r + 7, 1)], edge)
    edge = jnp.where(e == 2, rx_ref[pl.ds(r, 1)], edge)
    edge = jnp.where(e == 3, rx_ref[pl.ds(r + 1, 1)], edge)
    rows = ext_ref[pl.ds(r, 3)].reshape(384, channels)
    return jnp.concatenate([rows, edge.astype(BF16), jnp.zeros((112, channels), BF16)], axis=0)


def forward_band(wx_ref, mask_ref, r):
    weights = wx_ref[r + 1]
    same, ahead, back = mask_ref[0], mask_ref[1], mask_ref[2]
    bands = []
    for k in range(3):
        w = [line(weights, 7 * k + s) for s in range(7)]
        t = [tall(x) for x in w]
        spots = [mask_ref[4, 16 * n : 16 * n + 16] for n in range(4)]
        edge = spots[0] * w[2] + spots[1] * w[6] + spots[2] * w[1] + spots[3] * w[5]
        bands.append(
            jnp.concatenate(
                [
                    same * t[4] + back * t[6],
                    same * t[0] + ahead * t[1] + back * t[2],
                    same * t[3] + ahead * t[5],
                    edge,
                    jnp.zeros((112, 128), BF16),
                ],
                axis=0,
            )
        )
    return jnp.concatenate(bands, axis=1)


def transposed_band(wx_ref, we_ref, mask_ref, r):
    before, here, after = wx_ref[r], wx_ref[r + 1], wx_ref[r + 2]
    same, ahead, back = mask_ref[0], mask_ref[1], mask_ref[2]
    bands = []
    for k in range(3):
        at = lambda weights, slot: tall(line(weights, 7 * k + slot))
        beside = (
            we_ref[0, k, pl.ds(r + 8, 1)] + we_ref[1, k, pl.ds(r + 7, 1)] + we_ref[2, k, pl.ds(r + 9, 1)]
        )
        beside = jnp.broadcast_to(beside, (16, 128)).astype(BF16)
        bands.append(
            jnp.concatenate(
                [
                    same * at(before, 3) + ahead * at(before, 5),
                    same * at(here, 0) + ahead * at(here, 1) + back * at(here, 2),
                    same * at(after, 4) + back * at(after, 6),
                    mask_ref[3] * tall(beside),
                ],
                axis=1,
            )
        )
    return jnp.concatenate(bands, axis=0)


def spread(products):
    return [products[128 * k : 128 * k + 128].astype(BF16) for k in range(3)]


def gradient_kernel(
    ids_ref, f_ref, c_ref, stt_ref, above_ref, below_ref, left_ref, right_ref, tl_ref, br_ref,
    w1_ref, w2_ref,
    g_ref, up_ref, down_ref, gl_ref, gr_ref, ul_ref, dr_ref, keep_ref, send_ref,
    fext_ref, cext_ref, ff_ref, tt_ref, wx_ref, we_ref, flx_ref, frx_ref, clx_ref, crx_ref,
    mask_ref, total_ref, glx_ref, grx_ref,
):
    height, breadth, channels = f_ref.shape
    fill_masks(mask_ref)
    fill_weights(
        stt_ref, above_ref, below_ref, left_ref, right_ref, tl_ref, br_ref, wx_ref, we_ref
    )
    for which, (src, ext, lx, rx) in enumerate(
        ((f_ref, fext_ref, flx_ref, frx_ref), (c_ref, cext_ref, clx_ref, crx_ref))
    ):
        start = which * 2 * breadth
        ext[0] = whole(above_ref, start, breadth)
        ext[1 : 1 + height] = src[...]
        ext[1 + height] = whole(below_ref, start, breadth)
        side = which * 2 * height
        corner = lambda ref: jnp.concatenate(
            [ref[...].astype(F32)[2 * which : 2 * which + 1], ref[...].astype(F32)[2 * which + 1 : 2 * which + 2]],
            axis=1,
        )
        fill_sides(
            whole(left_ref, side, height), whole(right_ref, side, height), corner(tl_ref), corner(br_ref), lx, rx
        )

    @pl.loop(0, height)
    def _(r):
        rows = pl.ds(pl.multiple_of(r * 128, 128), 128)
        forward = dot(forward_band(wx_ref, mask_ref, r), field_block(fext_ref, flx_ref, frx_ref, r), 0, 0)
        ff_ref[rows] = jnp.concatenate([fext_ref[r + 1]] + spread(forward), axis=1)
        turned = dot(
            transposed_band(wx_ref, we_ref, mask_ref, r), field_block(cext_ref, clx_ref, crx_ref, r), 1, 0
        )
        tt_ref[rows] = jnp.concatenate([cext_ref[r + 1]] + spread(turned), axis=1)

    total_ref[...] = jnp.zeros_like(total_ref)
    batch = 4

    @pl.loop(0, height // batch)
    def _(i):
        rows = pl.ds(pl.multiple_of(i * batch * 128, batch * 128), batch * 128)
        pre = dot(ff_ref[rows], w1_ref[...], 1, 0)
        hidden_grad = dot(tt_ref[rows], w2_ref[...], 1, 0)
        gate = jax.nn.sigmoid(pre)
        hidden = (pre * gate).astype(BF16)
        grad = hidden_grad * gate * (1.0 + pre * (1.0 - gate))
        for q in range(batch):
            g_ref[i * batch + q] = grad[q * 128 : q * 128 + 128].astype(BF16)
            glx_ref[pl.ds(i * batch + q, 1)] = grad[q * 128 : q * 128 + 1]
            grx_ref[pl.ds(i * batch + q, 1)] = grad[q * 128 + 127 : q * 128 + 128]
        second = dot(hidden, tt_ref[rows], 0, 0)
        for k in range(4):
            total_ref[0, 4 * k : 4 * k + 4] += second[:, k * channels : (k + 1) * channels].reshape(
                4, channels // 4, channels
            )
        first = dot(ff_ref[rows], grad.astype(BF16), 0, 0)
        total_ref[1] += first.reshape(16, channels // 4, channels)

    up_ref[...] = g_ref[0]
    down_ref[...] = g_ref[height - 1]
    gl_ref[...] = glx_ref[...].astype(BF16)
    gr_ref[...] = grx_ref[...].astype(BF16)
    ul_ref[...] = jnp.broadcast_to(glx_ref[0:1], (16, channels)).astype(BF16)
    dr_ref[...] = jnp.broadcast_to(grx_ref[height - 1 : height], (16, channels)).astype(BF16)
    core, x, y = ids_ref[0], ids_ref[1], ids_ref[2]
    for dx in range(4):
        for dy in range(4):
            chunk = jnp.bitwise_xor(x, dx) * 4 + jnp.bitwise_xor(y, dy)
            keep_ref[4 * dx + dy] = total_ref[core, chunk]
            send_ref[4 * dx + dy] = total_ref[1 - core, chunk]


def input_kernel(
    g_ref, gabove_ref, gbelow_ref, gleft_ref, gright_ref, gtl_ref, gbr_ref,
    stt_ref, above_ref, below_ref, left_ref, right_ref, tl_ref, br_ref, w1t_ref,
    out_ref,
    gext_ref, tt_ref, wx_ref, we_ref, lx_ref, rx_ref, mask_ref,
):
    height, breadth, channels = g_ref.shape
    fill_masks(mask_ref)
    fill_weights(
        stt_ref, above_ref, below_ref, left_ref, right_ref, tl_ref, br_ref, wx_ref, we_ref
    )
    gext_ref[0] = gabove_ref[...]
    gext_ref[1 : 1 + height] = g_ref[...]
    gext_ref[1 + height] = gbelow_ref[...]
    fill_sides(
        gleft_ref[...], gright_ref[...], gtl_ref[...].astype(F32)[0:1], gbr_ref[...].astype(F32)[0:1], lx_ref, rx_ref
    )

    @pl.loop(0, height)
    def _(r):
        rows = pl.ds(pl.multiple_of(r * 128, 128), 128)
        turned = dot(
            transposed_band(wx_ref, we_ref, mask_ref, r), field_block(gext_ref, lx_ref, rx_ref, r), 1, 0
        )
        tt_ref[rows] = jnp.concatenate([gext_ref[r + 1]] + spread(turned), axis=1)

    batch = 4

    @pl.loop(0, height // batch)
    def _(i):
        rows = pl.ds(pl.multiple_of(i * batch * 128, batch * 128), batch * 128)
        result = dot(tt_ref[rows], w1t_ref[...], 1, 0).astype(BF16)
        for q in range(batch):
            out_ref[i * batch + q] = result[q * 128 : q * 128 + 128]


def final_kernel(scale, ids_ref, *refs):
    mine, theirs, out_refs = refs[:4], refs[4:8], refs[8:]
    core, x, y = ids_ref[0], ids_ref[1], ids_ref[2]
    first_core = core == 0
    for dx in range(4):
        for dy in range(4):
            chunk = jnp.bitwise_xor(x, dx) * 4 + jnp.bitwise_xor(y, dy)
            a = mine[dx][dy].astype(F32) * scale
            b = theirs[dx][dy].astype(F32) * scale
            out_refs[0][chunk] = jnp.where(first_core, a, b)
            out_refs[1][chunk] = jnp.where(first_core, b, a)


SMEM_SPEC = pl.BlockSpec(memory_space=pltpu.SMEM)
VMEM_SPEC = pl.BlockSpec(memory_space=pltpu.VMEM)


def gradients(ids, features, cotangent, stencil_t, rims, w1, w2t):
    height, breadth, channels = features.shape
    shape = jax.ShapeDtypeStruct
    totals = (16, channels // 4, channels)
    vertices = height * breadth
    return pl.pallas_call(
        gradient_kernel,
        out_shape=[
            shape((height, breadth, channels), BF16),
            shape((breadth, channels), BF16),
            shape((breadth, channels), BF16),
            shape((height, channels), BF16),
            shape((height, channels), BF16),
            shape((16, channels), BF16),
            shape((16, channels), BF16),
            shape(totals, F32),
            shape(totals, F32),
        ],
        in_specs=[SMEM_SPEC] + [VMEM_SPEC] * 11,
        scratch_shapes=[
            pltpu.VMEM((height + 2, breadth, channels), BF16),
            pltpu.VMEM((height + 2, breadth, channels), BF16),
            pltpu.VMEM((vertices, 4 * channels), BF16),
            pltpu.VMEM((vertices, 4 * channels), BF16),
            pltpu.VMEM((height + 2, SLOTS, 128), F32),
            pltpu.VMEM((3, 3, height + 16, 128), F32),
        ]
        + [pltpu.VMEM((height + 8, channels), F32)] * 4
        + [
            pltpu.VMEM((5, 128, 128), BF16),
            pltpu.VMEM((2,) + totals, F32),
            pltpu.VMEM((height, channels), F32),
            pltpu.VMEM((height, channels), F32),
        ],
        compiler_params=pltpu.CompilerParams(vmem_limit_bytes=VMEM_LIMIT),
        cost_estimate=pl.CostEstimate(flops=9 * 10**9, bytes_accessed=9 * 10**6, transcendentals=vertices * channels),
        name="weight_gradients",
    )(ids, features, cotangent, stencil_t, *rims, w1, w2t)


def input_gradient(grad, grad_rims, stencil_t, rims, w1t):
    height, breadth, channels = grad.shape
    return pl.pallas_call(
        input_kernel,
        out_shape=jax.ShapeDtypeStruct((height, breadth, channels), BF16),
        in_specs=[VMEM_SPEC] * 15,
        scratch_shapes=[
            pltpu.VMEM((height + 2, breadth, channels), BF16),
            pltpu.VMEM((height * breadth, 4 * channels), BF16),
            pltpu.VMEM((height + 2, SLOTS, 128), F32),
            pltpu.VMEM((3, 3, height + 16, 128), F32),
            pltpu.VMEM((height + 8, channels), F32),
            pltpu.VMEM((height + 8, channels), F32),
            pltpu.VMEM((5, 128, 128), BF16),
        ],
        compiler_params=pltpu.CompilerParams(vmem_limit_bytes=VMEM_LIMIT),
        cost_estimate=pl.CostEstimate(flops=3 * 10**9, bytes_accessed=3 * 10**6, transcendentals=0),
        name="input_gradient",
    )(grad, *grad_rims, stencil_t, *rims, w1t)


def swap(value, row_bits, col_bits):
    rows, cols = lax.axis_size("row"), lax.axis_size("col")
    pairs = [
        (r * cols + c, (r ^ row_bits) * cols + (c ^ col_bits)) for r in range(rows) for c in range(cols)
    ]
    return lax.ppermute(value, BOTH, pairs)


def reduce_both(keep, send):
    total = keep + swap(send, 0, 1)
    parts = [total[4 * d : 4 * d + 4] for d in range(4)]
    came = [swap(parts[d].astype(BF16), 4 * d, 0) for d in (1, 2, 3)]
    total = parts[0] + sum(v.astype(F32) for v in came)
    parts = [total[d] for d in range(4)]
    came = [swap(parts[d].astype(BF16), 0, 2 * d) for d in (1, 2, 3)]
    total = parts[0] + sum(v.astype(F32) for v in came)
    came = [swap(total, d, 0) for d in (1, 2, 3)]
    total = (total + came[0]) + (came[1] + came[2])
    total = (total + swap(total, 0, 8)).astype(BF16)
    gathered = jnp.stack([total] + [swap(total, 0, 2 * d) for d in (1, 2, 3)])
    mine = [gathered] + [swap(gathered, 4 * d, 0) for d in (1, 2, 3)]
    theirs = [swap(v, 0, 1) for v in mine]
    return mine, theirs


def body(features_in, stencil, weights_first, weights_second, cotangent):
    height, breadth, channels = features_in.shape
    scale = 1.0 / math.sqrt(height * breadth * lax.axis_size("row") * lax.axis_size("col"))
    flat = stencil.reshape(21, height, breadth)
    stencil_t = jnp.pad(flat.transpose(1, 0, 2), ((0, 0), (0, SLOTS - 21), (0, 0)))
    row, col = lax.axis_index("row"), lax.axis_index("col")
    ids = jnp.stack([col % 2, row // 4, (col // 2) % 4]).astype(jnp.int32)
    w1 = weights_first.reshape(4 * channels, channels)
    w1t = weights_first.transpose(0, 2, 1).reshape(4 * channels, channels)
    w2t = weights_second.transpose(0, 2, 1).reshape(4 * channels, channels)

    rims = exchange(pack(features_in, cotangent, flat, stencil_t), BOTH)
    grad, *messages, keep, send = gradients(ids, features_in, cotangent, stencil_t, rims, w1, w2t)
    mine, theirs = reduce_both(keep, send)
    input_grad = input_gradient(grad, exchange(messages, BOTH), stencil_t, rims, w1t)
    totals = jax.ShapeDtypeStruct((16, channels // 4, channels), F32)
    second, first = pl.pallas_call(
        functools.partial(final_kernel, scale),
        out_shape=[totals, totals],
        in_specs=[SMEM_SPEC] + [VMEM_SPEC] * 8,
        compiler_params=pltpu.CompilerParams(vmem_limit_bytes=VMEM_LIMIT),
        name="place_totals",
    )(ids, *mine, *theirs)
    shape = (4, channels, channels)
    return input_grad, first.reshape(shape), second.reshape(shape)


def solution(mesh):
    return jax.shard_map(
        body,
        mesh=mesh,
        in_specs=(
            P("row", "col", None),
            P(None, None, "row", "col"),
            P(),
            P(),
            P("row", "col", None),
        ),
        out_specs=(P("row", "col", None), P(), P()),
        check_vma=False,
    )
```

```python
import math

import jax
import jax.numpy as jnp
from jax import lax
from jax.experimental import pallas as pl
from jax.experimental.pallas import tpu as pltpu
from jax.sharding import PartitionSpec as P

F32 = jnp.float32
BF16 = jnp.bfloat16
BOTH = ("row", "col")
SLOTS = 32
VMEM_LIMIT = 56 * 1024 * 1024


def dot(lhs, rhs, lhs_dim, rhs_dim):
    return lax.dot_general(
        lhs, rhs, (((lhs_dim,), (rhs_dim,)), ((), ())), preferred_element_type=F32
    )


def iota(shape, dim):
    return lax.broadcasted_iota(jnp.int32, shape, dim)


def as_mask(condition):
    return jnp.where(condition, 1.0, 0.0).astype(BF16)


def halves(value):
    return jnp.concatenate([value[:, :128], value[:, 128:]], axis=0)


def whole(ref, start, rows):
    return jnp.concatenate([ref[start : start + rows], ref[start + rows : start + 2 * rows]], axis=1)


def even(axis):
    return lax.axis_index(axis) % 2 == 0


def choose(condition, value, other):
    return jnp.where(condition, value, other), jnp.where(condition, other, value)


def pack_kernel(f_ref, c_ref, st_ref, row0_ref, row1_ref, col0_ref, col1_ref):
    height, breadth, _ = f_ref.shape
    last = height - 1
    weights = st_ref[...].astype(F32)
    bottom_first = even("row")
    for out, first in ((row0_ref, True), (row1_ref, False)):
        row = jnp.where(bottom_first == first, last, 0)
        out[0 : 2 * breadth] = halves(f_ref[row])
        out[2 * breadth : 4 * breadth] = halves(c_ref[row])
    slots = [
        jnp.concatenate([weights[:, row, :], jnp.zeros((SLOTS - 21, 128), F32)], axis=0).astype(BF16)
        for row in (last, 0)
    ]
    ordered = choose(bottom_first, *slots)
    row0_ref[4 * breadth : 4 * breadth + SLOTS] = ordered[0]
    row1_ref[4 * breadth : 4 * breadth + SLOTS] = ordered[1]
    sides = []
    for col, first in ((breadth - 1, (1, 5)), (0, (2, 6))):
        base = 0 if col == 0 else breadth - 16
        parts = []
        for ref in (f_ref, c_ref):
            parts.append(halves(ref[:, base : base + 16, :].astype(F32)[:, col - base, :]).astype(BF16))
        parts += [st_ref[7 * k + slot] for slot in first for k in range(3)]
        sides.append(parts)
    start = 0
    for right, left in zip(*sides):
        rows = right.shape[0]
        col0_ref[start : start + rows], col1_ref[start : start + rows] = choose(even("col"), right, left)
        start += rows


def pack(features, cotangent, stencil):
    height, breadth, _ = features.shape
    sizes = (4 * breadth + SLOTS,) * 2 + (10 * height,) * 2
    return pl.pallas_call(
        pack_kernel,
        out_shape=[jax.ShapeDtypeStruct((n, 128), BF16) for n in sizes],
        compiler_params=pltpu.CompilerParams(vmem_limit_bytes=VMEM_LIMIT),
        name="pack_rims",
    )(features, cotangent, stencil)


def corner_kernel(row0_ref, row1_ref, col0_ref, col1_ref, out0_ref, out1_ref):
    size = col0_ref.shape[0]
    below, above = choose(even("row"), row0_ref[...].astype(F32), row1_ref[...].astype(F32))
    corners = []
    for rim, col, slot in ((above, 127, 5), (below, 0, 6)):
        lines = [rim[128 * n + col : 128 * n + col + 1] for n in range(4)]
        lines += [rim[512 + 7 * k + slot : 513 + 7 * k + slot] for k in range(3)]
        corners.append(jnp.concatenate(lines + [jnp.zeros((9, 128), F32)], axis=0).astype(BF16))
    out0_ref[0:size], out1_ref[0:size] = col0_ref[...], col1_ref[...]
    out0_ref[size : size + 16], out1_ref[size : size + 16] = choose(even("col"), *corners)


def grad_corner_kernel(row0_ref, row1_ref, col0_ref, col1_ref, out0_ref, out1_ref):
    size, channels = col0_ref.shape
    edges = []
    for ref in (row0_ref, row1_ref):
        value = ref[...].astype(F32)
        edges.append((value[0:1], value[127:128]))
    below = jnp.where(even("row"), edges[0][0], edges[1][0])
    above = jnp.where(even("row"), edges[1][1], edges[0][1])
    corners = [jnp.broadcast_to(v, (16, channels)).astype(BF16) for v in (above, below)]
    out0_ref[0:size], out1_ref[0:size] = col0_ref[...], col1_ref[...]
    out0_ref[size : size + 16], out1_ref[size : size + 16] = choose(even("col"), *corners)


def pair_swap(value, axis, offset):
    rows, cols = lax.axis_size("row"), lax.axis_size("col")
    pairs = []
    for r in range(rows):
        for c in range(cols):
            place = r if axis == "row" else c
            step = 1 if place % 2 == offset else -1
            to_r, to_c = (r + step, c) if axis == "row" else (r, (c + step) % cols)
            if 0 <= to_r < rows:
                pairs.append((r * cols + c, to_r * cols + to_c))
    return lax.ppermute(value, BOTH, pairs)


def exchange(row0, row1, col0, col1, kernel, name):
    row0, row1 = pair_swap(row0, "row", 0), pair_swap(row1, "row", 1)
    shape = (col0.shape[0] + 16, col0.shape[1])
    col0, col1 = pl.pallas_call(
        kernel, out_shape=[jax.ShapeDtypeStruct(shape, BF16)] * 2, name=name
    )(row0, row1, col0, col1)
    return row0, row1, pair_swap(col0, "col", 0), pair_swap(col1, "col", 1)


def place_rims(row0_ref, row1_ref, col0_ref, col1_ref, above_ref, below_ref, left_ref, right_ref):
    below_ref[...], above_ref[...] = choose(even("row"), row0_ref[...], row1_ref[...])
    right_ref[...], left_ref[...] = choose(even("col"), col0_ref[...], col1_ref[...])


def fill_masks(mask_ref):
    j, c = iota((128, 128), 0), iota((128, 128), 1)
    mask_ref[0] = as_mask(j == c)
    mask_ref[1] = as_mask(j == c + 1)
    mask_ref[2] = as_mask(j == c - 1)
    mask_ref[3] = as_mask(((j == 0) & (c < 2)) | ((j == 127) & ((c == 2) | (c == 3))))
    e, l = iota((16, 128), 0), iota((16, 128), 1)
    spots = ((0, 0), (1, 0), (2, 127), (3, 127))
    for number, (edge, lane) in enumerate(spots):
        mask_ref[4, 16 * number : 16 * number + 16] = as_mask((e == edge) & (l == lane))


def fill_weights(stt_ref, above_ref, below_ref, left_ref, right_ref, wx_ref, we_ref):
    height, _, breadth = stt_ref.shape
    base = 4 * breadth
    wx_ref[0] = above_ref[base : base + SLOTS].astype(F32)
    for r in range(height):
        wx_ref[1 + r] = stt_ref[r].astype(F32)
    wx_ref[height + 1] = below_ref[base : base + SLOTS].astype(F32)
    lane = iota((height, 128), 1)
    tl, br = left_ref[10 * height :], right_ref[10 * height :]

    def spot(value, shift, place):
        rolled = pltpu.roll(value.astype(F32), shift, 1)
        return jnp.where(lane[: value.shape[0]] == place, rolled, 0.0)

    for k in range(3):
        near = 4 * height + k * height
        far = near + 3 * height
        we_ref[0, k, 8 : 8 + height] = spot(left_ref[near : near + height], 1, 0) + spot(
            right_ref[near : near + height], 2, 2
        )
        we_ref[1, k, 8 : 8 + height] = spot(left_ref[far : far + height], 2, 1)
        we_ref[1, k, 0:8] = jnp.broadcast_to(spot(tl, 2, 1)[4 + k : 5 + k], (8, 128))
        we_ref[2, k, 8 : 8 + height] = spot(right_ref[far : far + height], 3, 3)
        we_ref[2, k, 8 + height : 16 + height] = jnp.broadcast_to(
            spot(br, 3, 3)[4 + k : 5 + k], (8, 128)
        )


def fill_sides(left, right, tl, br, lx_ref, rx_ref):
    height = left.shape[0]
    lx_ref[0:8] = jnp.broadcast_to(tl.astype(F32), (8, tl.shape[1]))
    lx_ref[8 : 8 + height] = left.astype(F32)
    rx_ref[0:height] = right.astype(F32)
    rx_ref[height : height + 8] = jnp.broadcast_to(br.astype(F32), (8, br.shape[1]))


def line(weights, slot):
    return jnp.broadcast_to(weights[slot : slot + 1], (16, 128)).astype(BF16)


def tall(value):
    return jnp.concatenate([value] * 8, axis=0)


def field_block(ext_ref, lx_ref, rx_ref, r):
    channels = ext_ref.shape[2]
    e = iota((16, channels), 0)
    edge = jnp.where(e == 0, lx_ref[pl.ds(r + 8, 1)], 0.0)
    edge = jnp.where(e == 1, lx_ref[pl.ds(r + 7, 1)], edge)
    edge = jnp.where(e == 2, rx_ref[pl.ds(r, 1)], edge)
    edge = jnp.where(e == 3, rx_ref[pl.ds(r + 1, 1)], edge)
    rows = ext_ref[pl.ds(r, 3)].reshape(384, channels)
    return jnp.concatenate([rows, edge.astype(BF16), jnp.zeros((112, channels), BF16)], axis=0)


def forward_band(wx_ref, mask_ref, r):
    weights = wx_ref[r + 1]
    same, ahead, back = mask_ref[0], mask_ref[1], mask_ref[2]
    bands = []
    for k in range(3):
        w = [line(weights, 7 * k + s) for s in range(7)]
        t = [tall(x) for x in w]
        spots = [mask_ref[4, 16 * n : 16 * n + 16] for n in range(4)]
        edge = spots[0] * w[2] + spots[1] * w[6] + spots[2] * w[1] + spots[3] * w[5]
        bands.append(
            jnp.concatenate(
                [
                    same * t[4] + back * t[6],
                    same * t[0] + ahead * t[1] + back * t[2],
                    same * t[3] + ahead * t[5],
                    edge,
                    jnp.zeros((112, 128), BF16),
                ],
                axis=0,
            )
        )
    return jnp.concatenate(bands, axis=1)


def transposed_band(wx_ref, we_ref, mask_ref, r):
    before, here, after = wx_ref[r], wx_ref[r + 1], wx_ref[r + 2]
    same, ahead, back = mask_ref[0], mask_ref[1], mask_ref[2]
    bands = []
    for k in range(3):
        at = lambda weights, slot: tall(line(weights, 7 * k + slot))
        beside = (
            we_ref[0, k, pl.ds(r + 8, 1)] + we_ref[1, k, pl.ds(r + 7, 1)] + we_ref[2, k, pl.ds(r + 9, 1)]
        )
        beside = jnp.broadcast_to(beside, (16, 128)).astype(BF16)
        bands.append(
            jnp.concatenate(
                [
                    same * at(before, 3) + ahead * at(before, 5),
                    same * at(here, 0) + ahead * at(here, 1) + back * at(here, 2),
                    same * at(after, 4) + back * at(after, 6),
                    mask_ref[3] * tall(beside),
                ],
                axis=1,
            )
        )
    return jnp.concatenate(bands, axis=0)


def spread(products):
    return [products[128 * k : 128 * k + 128].astype(BF16) for k in range(3)]


def gradient_kernel(
    f_ref, c_ref, stt_ref, row0_ref, row1_ref, col0_ref, col1_ref, w1_ref, w2_ref,
    g_ref, grow0_ref, grow1_ref, gcol0_ref, gcol1_ref, keep_ref, send_ref,
    above_ref, below_ref, left_ref, right_ref,
    fext_ref, cext_ref, ff_ref, tt_ref, wx_ref, we_ref, flx_ref, frx_ref, clx_ref, crx_ref,
    mask_ref, total_ref, glx_ref, grx_ref,
):
    height, breadth, channels = f_ref.shape
    fill_masks(mask_ref)
    place_rims(row0_ref, row1_ref, col0_ref, col1_ref, above_ref, below_ref, left_ref, right_ref)
    fill_weights(stt_ref, above_ref, below_ref, left_ref, right_ref, wx_ref, we_ref)
    for which, (src, ext, lx, rx) in enumerate(
        ((f_ref, fext_ref, flx_ref, frx_ref), (c_ref, cext_ref, clx_ref, crx_ref))
    ):
        start = which * 2 * breadth
        ext[0] = whole(above_ref, start, breadth)
        ext[1 : 1 + height] = src[...]
        ext[1 + height] = whole(below_ref, start, breadth)
        side = which * 2 * height
        lines = lambda ref: ref[10 * height :].astype(F32)[2 * which : 2 * which + 2]
        corner = lambda ref: jnp.concatenate([lines(ref)[0:1], lines(ref)[1:2]], axis=1)
        fill_sides(
            whole(left_ref, side, height), whole(right_ref, side, height), corner(left_ref), corner(right_ref), lx, rx
        )

    @pl.loop(0, height)
    def _(r):
        rows = pl.ds(pl.multiple_of(r * 128, 128), 128)
        forward = dot(forward_band(wx_ref, mask_ref, r), field_block(fext_ref, flx_ref, frx_ref, r), 0, 0)
        ff_ref[rows] = jnp.concatenate([fext_ref[r + 1]] + spread(forward), axis=1)
        turned = dot(
            transposed_band(wx_ref, we_ref, mask_ref, r), field_block(cext_ref, clx_ref, crx_ref, r), 1, 0
        )
        tt_ref[rows] = jnp.concatenate([cext_ref[r + 1]] + spread(turned), axis=1)

    total_ref[...] = jnp.zeros_like(total_ref)
    batch = 4

    @pl.loop(0, height // batch)
    def _(i):
        rows = pl.ds(pl.multiple_of(i * batch * 128, batch * 128), batch * 128)
        pre = dot(ff_ref[rows], w1_ref[...], 1, 0)
        hidden_grad = dot(tt_ref[rows], w2_ref[...], 1, 0)
        gate = jax.nn.sigmoid(pre)
        hidden = (pre * gate).astype(BF16)
        grad = hidden_grad * gate * (1.0 + pre * (1.0 - gate))
        for q in range(batch):
            g_ref[i * batch + q] = grad[q * 128 : q * 128 + 128].astype(BF16)
            glx_ref[pl.ds(i * batch + q, 1)] = grad[q * 128 : q * 128 + 1]
            grx_ref[pl.ds(i * batch + q, 1)] = grad[q * 128 + 127 : q * 128 + 128]
        second = dot(hidden, tt_ref[rows], 0, 0)
        for k in range(4):
            total_ref[0, 4 * k : 4 * k + 4] += second[:, k * channels : (k + 1) * channels].reshape(
                4, channels // 4, channels
            )
        first = dot(ff_ref[rows], grad.astype(BF16), 0, 0)
        total_ref[1] += first.reshape(16, channels // 4, channels)

    grow0_ref[...], grow1_ref[...] = choose(even("row"), g_ref[height - 1], g_ref[0])
    gcol0_ref[...], gcol1_ref[...] = choose(
        even("col"), grx_ref[...].astype(BF16), glx_ref[...].astype(BF16)
    )
    core = lax.axis_index("col") % 2
    keep_ref[...] = total_ref[core]
    send_ref[...] = total_ref[1 - core]


def input_kernel(
    g_ref, grow0_ref, grow1_ref, gcol0_ref, gcol1_ref,
    stt_ref, row0_ref, row1_ref, col0_ref, col1_ref, w1t_ref,
    out_ref,
    above_ref, below_ref, left_ref, right_ref,
    gext_ref, tt_ref, wx_ref, we_ref, lx_ref, rx_ref, mask_ref,
):
    height, breadth, channels = g_ref.shape
    fill_masks(mask_ref)
    place_rims(row0_ref, row1_ref, col0_ref, col1_ref, above_ref, below_ref, left_ref, right_ref)
    fill_weights(stt_ref, above_ref, below_ref, left_ref, right_ref, wx_ref, we_ref)
    gext_ref[1 + height], gext_ref[0] = choose(even("row"), grow0_ref[...], grow1_ref[...])
    gext_ref[1 : 1 + height] = g_ref[...]
    right, left = choose(even("col"), gcol0_ref[...], gcol1_ref[...])
    corner = lambda value: value[height:].astype(F32)[0:1]
    fill_sides(left[:height], right[:height], corner(left), corner(right), lx_ref, rx_ref)

    @pl.loop(0, height)
    def _(r):
        rows = pl.ds(pl.multiple_of(r * 128, 128), 128)
        turned = dot(
            transposed_band(wx_ref, we_ref, mask_ref, r), field_block(gext_ref, lx_ref, rx_ref, r), 1, 0
        )
        tt_ref[rows] = jnp.concatenate([gext_ref[r + 1]] + spread(turned), axis=1)

    batch = 4

    @pl.loop(0, height // batch)
    def _(i):
        rows = pl.ds(pl.multiple_of(i * batch * 128, batch * 128), batch * 128)
        result = dot(tt_ref[rows], w1t_ref[...], 1, 0).astype(BF16)
        for q in range(batch):
            out_ref[i * batch + q] = result[q * 128 : q * 128 + 128]


VMEM_SPEC = pl.BlockSpec(memory_space=pltpu.VMEM)


def gradients(features, cotangent, stencil_t, rims, w1, w2t):
    height, breadth, channels = features.shape
    shape = jax.ShapeDtypeStruct
    totals = (16, channels // 4, channels)
    vertices = height * breadth
    return pl.pallas_call(
        gradient_kernel,
        out_shape=[
            shape((height, breadth, channels), BF16),
            shape((breadth, channels), BF16),
            shape((breadth, channels), BF16),
            shape((height, channels), BF16),
            shape((height, channels), BF16),
            shape(totals, F32),
            shape(totals, F32),
        ],
        in_specs=[VMEM_SPEC] * 9,
        scratch_shapes=[pltpu.VMEM(v.shape, BF16) for v in rims]
        + [
            pltpu.VMEM((height + 2, breadth, channels), BF16),
            pltpu.VMEM((height + 2, breadth, channels), BF16),
            pltpu.VMEM((vertices, 4 * channels), BF16),
            pltpu.VMEM((vertices, 4 * channels), BF16),
            pltpu.VMEM((height + 2, SLOTS, 128), F32),
            pltpu.VMEM((3, 3, height + 16, 128), F32),
        ]
        + [pltpu.VMEM((height + 8, channels), F32)] * 4
        + [
            pltpu.VMEM((5, 128, 128), BF16),
            pltpu.VMEM((2,) + totals, F32),
            pltpu.VMEM((height, channels), F32),
            pltpu.VMEM((height, channels), F32),
        ],
        compiler_params=pltpu.CompilerParams(vmem_limit_bytes=VMEM_LIMIT),
        cost_estimate=pl.CostEstimate(flops=9 * 10**9, bytes_accessed=9 * 10**6, transcendentals=vertices * channels),
        name="weight_gradients",
    )(features, cotangent, stencil_t, *rims, w1, w2t)


def input_gradient(grad, grad_rims, stencil_t, rims, w1t):
    height, breadth, channels = grad.shape
    return pl.pallas_call(
        input_kernel,
        out_shape=jax.ShapeDtypeStruct((height, breadth, channels), BF16),
        in_specs=[VMEM_SPEC] * 11,
        scratch_shapes=[pltpu.VMEM(v.shape, BF16) for v in rims]
        + [
            pltpu.VMEM((height + 2, breadth, channels), BF16),
            pltpu.VMEM((height * breadth, 4 * channels), BF16),
            pltpu.VMEM((height + 2, SLOTS, 128), F32),
            pltpu.VMEM((3, 3, height + 16, 128), F32),
            pltpu.VMEM((height + 8, channels), F32),
            pltpu.VMEM((height + 8, channels), F32),
            pltpu.VMEM((5, 128, 128), BF16),
        ],
        compiler_params=pltpu.CompilerParams(vmem_limit_bytes=VMEM_LIMIT),
        cost_estimate=pl.CostEstimate(flops=3 * 10**9, bytes_accessed=3 * 10**6, transcendentals=0),
        name="input_gradient",
    )(grad, *grad_rims, stencil_t, *rims, w1t)


def swap(value, row_bits, col_bits):
    rows, cols = lax.axis_size("row"), lax.axis_size("col")
    pairs = [
        (r * cols + c, (r ^ row_bits) * cols + (c ^ col_bits)) for r in range(rows) for c in range(cols)
    ]
    return lax.ppermute(value, BOTH, pairs)


def reduce_both(keep, send):
    cols = lax.axis_size("col")
    planes = [
        [cols * (4 * x + z) + 8 * h + 2 * y + core for x in range(4) for y in range(4)]
        for z in range(4)
        for h in range(2)
        for core in range(2)
    ]
    trade = lambda v: lax.all_to_all(v, BOTH, 0, 0, axis_index_groups=planes, tiled=True)
    total = trade((keep + swap(send, 0, 1)).astype(BF16)).astype(F32).sum(0)
    came = [swap(total, d, 0) for d in (1, 2, 3)]
    total = (total + came[0]) + (came[1] + came[2])
    total = (total + swap(total, 3, 8)).astype(BF16)
    mine = trade(jnp.broadcast_to(total[None], keep.shape))
    return mine, swap(mine, 0, 1)


def body(features_in, stencil, weights_first, weights_second, cotangent):
    height, breadth, channels = features_in.shape
    scale = 1.0 / math.sqrt(height * breadth * lax.axis_size("row") * lax.axis_size("col"))
    flat = stencil.reshape(21, height, breadth)
    stencil_t = jnp.pad(flat.transpose(1, 0, 2), ((0, 0), (0, SLOTS - 21), (0, 0)))
    w1 = weights_first.reshape(4 * channels, channels)
    w1t = weights_first.transpose(0, 2, 1).reshape(4 * channels, channels)
    w2t = weights_second.transpose(0, 2, 1).reshape(4 * channels, channels)

    rims = exchange(*pack(features_in, cotangent, flat), corner_kernel, "pack_corners")
    grad, *messages, keep, send = gradients(features_in, cotangent, stencil_t, rims, w1, w2t)
    mine, theirs = reduce_both(keep, send)
    grad_rims = exchange(*messages, grad_corner_kernel, "pack_grad_corners")
    input_grad = input_gradient(grad, grad_rims, stencil_t, rims, w1t)
    mine, theirs = mine.astype(F32) * scale, theirs.astype(F32) * scale
    second = jnp.where(even("col"), mine, theirs).reshape(4, channels, channels)
    first = jnp.where(even("col"), theirs, mine).reshape(4, channels, channels)
    return input_grad, first, second


def solution(mesh):
    return jax.shard_map(
        body,
        mesh=mesh,
        in_specs=(
            P("row", "col", None),
            P(None, None, "row", "col"),
            P(),
            P(),
            P("row", "col", None),
        ),
        out_specs=(P("row", "col", None), P(), P()),
        check_vma=False,
    )
```

```python
import math

import jax
import jax.numpy as jnp
from jax import lax
from jax.experimental import pallas as pl
from jax.experimental.pallas import tpu as pltpu
from jax.sharding import PartitionSpec as P

F32 = jnp.float32
BF16 = jnp.bfloat16
BOTH = ("row", "col")
SLOTS = 32
VMEM_LIMIT = 28 * 1024 * 1024


def dot(lhs, rhs, lhs_dim, rhs_dim):
    return lax.dot_general(
        lhs, rhs, (((lhs_dim,), (rhs_dim,)), ((), ())), preferred_element_type=F32
    )


def iota(shape, dim):
    return lax.broadcasted_iota(jnp.int32, shape, dim)


def as_mask(condition):
    return jnp.where(condition, 1.0, 0.0).astype(BF16)


def halves(value):
    return jnp.concatenate([value[:, :128], value[:, 128:]], axis=0)


def whole(ref, start, rows):
    return jnp.concatenate([ref[start : start + rows], ref[start + rows : start + 2 * rows]], axis=1)


def even(axis):
    return lax.axis_index(axis) % 2 == 0


def choose(condition, value, other):
    return jnp.where(condition, value, other), jnp.where(condition, other, value)


def pack_kernel(f_ref, c_ref, st_ref, row0_ref, row1_ref, col0_ref, col1_ref):
    height, breadth, _ = f_ref.shape
    last = height - 1
    weights = st_ref[...].astype(F32)
    bottom_first = even("row")
    for out, first in ((row0_ref, True), (row1_ref, False)):
        row = jnp.where(bottom_first == first, last, 0)
        out[0 : 2 * breadth] = halves(f_ref[row])
        out[2 * breadth : 4 * breadth] = halves(c_ref[row])
    slots = [
        jnp.concatenate([weights[:, row, :], jnp.zeros((SLOTS - 21, 128), F32)], axis=0).astype(BF16)
        for row in (last, 0)
    ]
    ordered = choose(bottom_first, *slots)
    row0_ref[4 * breadth : 4 * breadth + SLOTS] = ordered[0]
    row1_ref[4 * breadth : 4 * breadth + SLOTS] = ordered[1]
    sides = []
    for col, first in ((breadth - 1, (1, 5)), (0, (2, 6))):
        base = 0 if col == 0 else breadth - 16
        parts = []
        for ref in (f_ref, c_ref):
            parts.append(halves(ref[:, base : base + 16, :].astype(F32)[:, col - base, :]).astype(BF16))
        parts += [st_ref[7 * k + slot] for slot in first for k in range(3)]
        sides.append(parts)
    start = 0
    for right, left in zip(*sides):
        rows = right.shape[0]
        col0_ref[start : start + rows], col1_ref[start : start + rows] = choose(even("col"), right, left)
        start += rows


def pack(features, cotangent, stencil):
    height, breadth, _ = features.shape
    sizes = (4 * breadth + SLOTS,) * 2 + (10 * height,) * 2
    return pl.pallas_call(
        pack_kernel,
        out_shape=[jax.ShapeDtypeStruct((n, 128), BF16) for n in sizes],
        compiler_params=pltpu.CompilerParams(vmem_limit_bytes=VMEM_LIMIT),
        name="pack_rims",
    )(features, cotangent, stencil)


def corner_kernel(row0_ref, row1_ref, col0_ref, col1_ref, out0_ref, out1_ref):
    size = col0_ref.shape[0]
    below, above = choose(even("row"), row0_ref[...].astype(F32), row1_ref[...].astype(F32))
    corners = []
    for rim, col, slot in ((above, 127, 5), (below, 0, 6)):
        lines = [rim[128 * n + col : 128 * n + col + 1] for n in range(4)]
        lines += [rim[512 + 7 * k + slot : 513 + 7 * k + slot] for k in range(3)]
        corners.append(jnp.concatenate(lines + [jnp.zeros((9, 128), F32)], axis=0).astype(BF16))
    out0_ref[0:size], out1_ref[0:size] = col0_ref[...], col1_ref[...]
    out0_ref[size : size + 16], out1_ref[size : size + 16] = choose(even("col"), *corners)


def grad_corner_kernel(row0_ref, row1_ref, col0_ref, col1_ref, out0_ref, out1_ref):
    size, channels = col0_ref.shape
    edges = []
    for ref in (row0_ref, row1_ref):
        value = ref[...].astype(F32)
        edges.append((value[0:1], value[127:128]))
    below = jnp.where(even("row"), edges[0][0], edges[1][0])
    above = jnp.where(even("row"), edges[1][1], edges[0][1])
    corners = [jnp.broadcast_to(v, (16, channels)).astype(BF16) for v in (above, below)]
    out0_ref[0:size], out1_ref[0:size] = col0_ref[...], col1_ref[...]
    out0_ref[size : size + 16], out1_ref[size : size + 16] = choose(even("col"), *corners)


def pair_swap(value, axis, offset):
    rows, cols = lax.axis_size("row"), lax.axis_size("col")
    pairs = []
    for r in range(rows):
        for c in range(cols):
            place = r if axis == "row" else c
            step = 1 if place % 2 == offset else -1
            to_r, to_c = (r + step, c) if axis == "row" else (r, (c + step) % cols)
            if 0 <= to_r < rows:
                pairs.append((r * cols + c, to_r * cols + to_c))
    return lax.ppermute(value, BOTH, pairs)


def add_corners(row0, row1, col0, col1, kernel, name):
    shape = (col0.shape[0] + 16, col0.shape[1])
    return pl.pallas_call(kernel, out_shape=[jax.ShapeDtypeStruct(shape, BF16)] * 2, name=name)(
        row0, row1, col0, col1
    )


def exchange(row0, row1, col0, col1, kernel, name):
    row0, row1 = pair_swap(row0, "row", 0), pair_swap(row1, "row", 1)
    col0, col1 = add_corners(row0, row1, col0, col1, kernel, name)
    return row0, row1, pair_swap(col0, "col", 0), pair_swap(col1, "col", 1)


def place_rims(row0_ref, row1_ref, col0_ref, col1_ref, above_ref, below_ref, left_ref, right_ref):
    below_ref[...], above_ref[...] = choose(even("row"), row0_ref[...], row1_ref[...])
    right_ref[...], left_ref[...] = choose(even("col"), col0_ref[...], col1_ref[...])


def fill_masks(mask_ref):
    j, c = iota((128, 128), 0), iota((128, 128), 1)
    mask_ref[0] = as_mask(j == c)
    mask_ref[1] = as_mask(j == c + 1)
    mask_ref[2] = as_mask(j == c - 1)
    mask_ref[3] = as_mask(((j == 0) & (c < 2)) | ((j == 127) & ((c == 2) | (c == 3))))
    e, l = iota((16, 128), 0), iota((16, 128), 1)
    spots = ((0, 0), (1, 0), (2, 127), (3, 127))
    for number, (edge, lane) in enumerate(spots):
        mask_ref[4, 16 * number : 16 * number + 16] = as_mask((e == edge) & (l == lane))


def fill_weights(stt_ref, above_ref, below_ref, left_ref, right_ref, wx_ref, we_ref):
    height, _, breadth = stt_ref.shape
    base = 4 * breadth
    wx_ref[0] = above_ref[base : base + SLOTS].astype(F32)
    for r in range(height):
        wx_ref[1 + r] = stt_ref[r].astype(F32)
    wx_ref[height + 1] = below_ref[base : base + SLOTS].astype(F32)
    lane = iota((height, 128), 1)
    tl, br = left_ref[10 * height :], right_ref[10 * height :]

    def spot(value, shift, place):
        rolled = pltpu.roll(value.astype(F32), shift, 1)
        return jnp.where(lane[: value.shape[0]] == place, rolled, 0.0)

    for k in range(3):
        near = 4 * height + k * height
        far = near + 3 * height
        we_ref[0, k, 8 : 8 + height] = spot(left_ref[near : near + height], 1, 0) + spot(
            right_ref[near : near + height], 2, 2
        )
        we_ref[1, k, 8 : 8 + height] = spot(left_ref[far : far + height], 2, 1)
        we_ref[1, k, 0:8] = jnp.broadcast_to(spot(tl, 2, 1)[4 + k : 5 + k], (8, 128))
        we_ref[2, k, 8 : 8 + height] = spot(right_ref[far : far + height], 3, 3)
        we_ref[2, k, 8 + height : 16 + height] = jnp.broadcast_to(
            spot(br, 3, 3)[4 + k : 5 + k], (8, 128)
        )


def fill_sides(left, right, tl, br, lx_ref, rx_ref):
    height = left.shape[0]
    lx_ref[0:8] = jnp.broadcast_to(tl.astype(F32), (8, tl.shape[1]))
    lx_ref[8 : 8 + height] = left.astype(F32)
    rx_ref[0:height] = right.astype(F32)
    rx_ref[height : height + 8] = jnp.broadcast_to(br.astype(F32), (8, br.shape[1]))


def line(weights, slot):
    return jnp.broadcast_to(weights[slot : slot + 1], (16, 128)).astype(BF16)


def tall(value):
    return jnp.concatenate([value] * 8, axis=0)


def field_block(ext_ref, lx_ref, rx_ref, r):
    channels = ext_ref.shape[2]
    e = iota((16, channels), 0)
    edge = jnp.where(e == 0, lx_ref[pl.ds(r + 8, 1)], 0.0)
    edge = jnp.where(e == 1, lx_ref[pl.ds(r + 7, 1)], edge)
    edge = jnp.where(e == 2, rx_ref[pl.ds(r, 1)], edge)
    edge = jnp.where(e == 3, rx_ref[pl.ds(r + 1, 1)], edge)
    rows = ext_ref[pl.ds(r, 3)].reshape(384, channels)
    return jnp.concatenate([rows, edge.astype(BF16), jnp.zeros((112, channels), BF16)], axis=0)


def forward_band(wx_ref, mask_ref, r):
    weights = wx_ref[r + 1]
    same, ahead, back = mask_ref[0], mask_ref[1], mask_ref[2]
    bands = []
    for k in range(3):
        w = [line(weights, 7 * k + s) for s in range(7)]
        t = [tall(x) for x in w]
        spots = [mask_ref[4, 16 * n : 16 * n + 16] for n in range(4)]
        edge = spots[0] * w[2] + spots[1] * w[6] + spots[2] * w[1] + spots[3] * w[5]
        bands.append(
            jnp.concatenate(
                [
                    same * t[4] + back * t[6],
                    same * t[0] + ahead * t[1] + back * t[2],
                    same * t[3] + ahead * t[5],
                    edge,
                    jnp.zeros((112, 128), BF16),
                ],
                axis=0,
            )
        )
    return jnp.concatenate(bands, axis=1)


def transposed_band(wx_ref, we_ref, mask_ref, r):
    before, here, after = wx_ref[r], wx_ref[r + 1], wx_ref[r + 2]
    same, ahead, back = mask_ref[0], mask_ref[1], mask_ref[2]
    bands = []
    for k in range(3):
        at = lambda weights, slot: tall(line(weights, 7 * k + slot))
        beside = (
            we_ref[0, k, pl.ds(r + 8, 1)] + we_ref[1, k, pl.ds(r + 7, 1)] + we_ref[2, k, pl.ds(r + 9, 1)]
        )
        beside = jnp.broadcast_to(beside, (16, 128)).astype(BF16)
        bands.append(
            jnp.concatenate(
                [
                    same * at(before, 3) + ahead * at(before, 5),
                    same * at(here, 0) + ahead * at(here, 1) + back * at(here, 2),
                    same * at(after, 4) + back * at(after, 6),
                    mask_ref[3] * tall(beside),
                ],
                axis=1,
            )
        )
    return jnp.concatenate(bands, axis=0)


def spread(products):
    return [products[128 * k : 128 * k + 128].astype(BF16) for k in range(3)]


def gradient_kernel(
    f_ref, c_ref, stt_ref, row0_ref, row1_ref, col0_ref, col1_ref, w1_ref, w2_ref,
    g_ref, grow0_ref, grow1_ref, gcol0_ref, gcol1_ref, keep_ref, send_ref,
    above_ref, below_ref, left_ref, right_ref,
    fext_ref, cext_ref, ff_ref, tt_ref, wx_ref, we_ref, flx_ref, frx_ref, clx_ref, crx_ref,
    mask_ref, total_ref, glx_ref, grx_ref,
):
    height, breadth, channels = f_ref.shape
    fill_masks(mask_ref)
    place_rims(row0_ref, row1_ref, col0_ref, col1_ref, above_ref, below_ref, left_ref, right_ref)
    fill_weights(stt_ref, above_ref, below_ref, left_ref, right_ref, wx_ref, we_ref)
    for which, (src, ext, lx, rx) in enumerate(
        ((f_ref, fext_ref, flx_ref, frx_ref), (c_ref, cext_ref, clx_ref, crx_ref))
    ):
        start = which * 2 * breadth
        ext[0] = whole(above_ref, start, breadth)
        ext[1 : 1 + height] = src[...]
        ext[1 + height] = whole(below_ref, start, breadth)
        side = which * 2 * height
        lines = lambda ref: ref[10 * height :].astype(F32)[2 * which : 2 * which + 2]
        corner = lambda ref: jnp.concatenate([lines(ref)[0:1], lines(ref)[1:2]], axis=1)
        fill_sides(
            whole(left_ref, side, height), whole(right_ref, side, height), corner(left_ref), corner(right_ref), lx, rx
        )

    @pl.loop(0, height, unroll=8)
    def _(r):
        rows = pl.ds(pl.multiple_of(r * 128, 128), 128)
        forward = dot(forward_band(wx_ref, mask_ref, r), field_block(fext_ref, flx_ref, frx_ref, r), 0, 0)
        ff_ref[rows] = jnp.concatenate([fext_ref[r + 1]] + spread(forward), axis=1)
        turned = dot(
            transposed_band(wx_ref, we_ref, mask_ref, r), field_block(cext_ref, clx_ref, crx_ref, r), 1, 0
        )
        tt_ref[rows] = jnp.concatenate([cext_ref[r + 1]] + spread(turned), axis=1)

    total_ref[...] = jnp.zeros_like(total_ref)
    batch = 4

    @pl.loop(0, height // batch)
    def _(i):
        rows = pl.ds(pl.multiple_of(i * batch * 128, batch * 128), batch * 128)
        pre = dot(ff_ref[rows], w1_ref[...], 1, 0)
        hidden_grad = dot(tt_ref[rows], w2_ref[...], 1, 0)
        gate = jax.nn.sigmoid(pre)
        hidden = (pre * gate).astype(BF16)
        grad = hidden_grad * gate * (1.0 + pre * (1.0 - gate))
        for q in range(batch):
            g_ref[i * batch + q] = grad[q * 128 : q * 128 + 128].astype(BF16)
            glx_ref[pl.ds(i * batch + q, 1)] = grad[q * 128 : q * 128 + 1]
            grx_ref[pl.ds(i * batch + q, 1)] = grad[q * 128 + 127 : q * 128 + 128]
        second = dot(hidden, tt_ref[rows], 0, 0)
        for k in range(4):
            total_ref[0, 4 * k : 4 * k + 4] += second[:, k * channels : (k + 1) * channels].reshape(
                4, channels // 4, channels
            )
        first = dot(ff_ref[rows], grad.astype(BF16), 0, 0)
        total_ref[1] += first.reshape(16, channels // 4, channels)

    grow0_ref[...], grow1_ref[...] = choose(even("row"), g_ref[height - 1], g_ref[0])
    gcol0_ref[...], gcol1_ref[...] = choose(
        even("col"), grx_ref[...].astype(BF16), glx_ref[...].astype(BF16)
    )
    core = lax.axis_index("col") % 2
    keep_ref[...] = total_ref[core]
    send_ref[...] = total_ref[1 - core]


def input_kernel(
    g_ref, grow0_ref, grow1_ref, gcol0_ref, gcol1_ref,
    stt_ref, row0_ref, row1_ref, col0_ref, col1_ref, w1t_ref,
    out_ref,
    above_ref, below_ref, left_ref, right_ref,
    gext_ref, tt_ref, wx_ref, we_ref, lx_ref, rx_ref, mask_ref,
):
    height, breadth, channels = g_ref.shape
    fill_masks(mask_ref)
    place_rims(row0_ref, row1_ref, col0_ref, col1_ref, above_ref, below_ref, left_ref, right_ref)
    fill_weights(stt_ref, above_ref, below_ref, left_ref, right_ref, wx_ref, we_ref)
    gext_ref[1 + height], gext_ref[0] = choose(even("row"), grow0_ref[...], grow1_ref[...])
    gext_ref[1 : 1 + height] = g_ref[...]
    right, left = choose(even("col"), gcol0_ref[...], gcol1_ref[...])
    corner = lambda value: value[height:].astype(F32)[0:1]
    fill_sides(left[:height], right[:height], corner(left), corner(right), lx_ref, rx_ref)

    @pl.loop(0, height, unroll=8)
    def _(r):
        rows = pl.ds(pl.multiple_of(r * 128, 128), 128)
        turned = dot(
            transposed_band(wx_ref, we_ref, mask_ref, r), field_block(gext_ref, lx_ref, rx_ref, r), 1, 0
        )
        tt_ref[rows] = jnp.concatenate([gext_ref[r + 1]] + spread(turned), axis=1)

    batch = 4

    @pl.loop(0, height // batch)
    def _(i):
        rows = pl.ds(pl.multiple_of(i * batch * 128, batch * 128), batch * 128)
        result = dot(tt_ref[rows], w1t_ref[...], 1, 0).astype(BF16)
        for q in range(batch):
            out_ref[i * batch + q] = result[q * 128 : q * 128 + 128]


VMEM_SPEC = pl.BlockSpec(memory_space=pltpu.VMEM)


def gradients(features, cotangent, stencil_t, rims, w1, w2t):
    height, breadth, channels = features.shape
    shape = jax.ShapeDtypeStruct
    totals = (16, channels // 4, channels)
    vertices = height * breadth
    return pl.pallas_call(
        gradient_kernel,
        out_shape=[
            shape((height, breadth, channels), BF16),
            shape((breadth, channels), BF16),
            shape((breadth, channels), BF16),
            shape((height, channels), BF16),
            shape((height, channels), BF16),
            shape(totals, F32),
            shape(totals, F32),
        ],
        in_specs=[VMEM_SPEC] * 9,
        scratch_shapes=[pltpu.VMEM(v.shape, BF16) for v in rims]
        + [
            pltpu.VMEM((height + 2, breadth, channels), BF16),
            pltpu.VMEM((height + 2, breadth, channels), BF16),
            pltpu.VMEM((vertices, 4 * channels), BF16),
            pltpu.VMEM((vertices, 4 * channels), BF16),
            pltpu.VMEM((height + 2, SLOTS, 128), F32),
            pltpu.VMEM((3, 3, height + 16, 128), F32),
        ]
        + [pltpu.VMEM((height + 8, channels), F32)] * 4
        + [
            pltpu.VMEM((5, 128, 128), BF16),
            pltpu.VMEM((2,) + totals, F32),
            pltpu.VMEM((height, channels), F32),
            pltpu.VMEM((height, channels), F32),
        ],
        compiler_params=pltpu.CompilerParams(vmem_limit_bytes=VMEM_LIMIT),
        cost_estimate=pl.CostEstimate(flops=9 * 10**9, bytes_accessed=9 * 10**6, transcendentals=vertices * channels),
        name="weight_gradients",
    )(features, cotangent, stencil_t, *rims, w1, w2t)


def input_gradient(grad, grad_rims, stencil_t, rims, w1t):
    height, breadth, channels = grad.shape
    return pl.pallas_call(
        input_kernel,
        out_shape=jax.ShapeDtypeStruct((height, breadth, channels), BF16),
        in_specs=[VMEM_SPEC] * 11,
        scratch_shapes=[pltpu.VMEM(v.shape, BF16) for v in rims]
        + [
            pltpu.VMEM((height + 2, breadth, channels), BF16),
            pltpu.VMEM((height * breadth, 4 * channels), BF16),
            pltpu.VMEM((height + 2, SLOTS, 128), F32),
            pltpu.VMEM((3, 3, height + 16, 128), F32),
            pltpu.VMEM((height + 8, channels), F32),
            pltpu.VMEM((height + 8, channels), F32),
            pltpu.VMEM((5, 128, 128), BF16),
        ],
        compiler_params=pltpu.CompilerParams(vmem_limit_bytes=VMEM_LIMIT),
        cost_estimate=pl.CostEstimate(flops=3 * 10**9, bytes_accessed=3 * 10**6, transcendentals=0),
        name="input_gradient",
    )(grad, *grad_rims, stencil_t, *rims, w1t)


def swap(value, row_bits, col_bits):
    rows, cols = lax.axis_size("row"), lax.axis_size("col")
    pairs = [
        (r * cols + c, (r ^ row_bits) * cols + (c ^ col_bits)) for r in range(rows) for c in range(cols)
    ]
    return lax.ppermute(value, BOTH, pairs)


def plane_trade(value):
    cols = lax.axis_size("col")
    planes = [
        [cols * (4 * x + z) + 8 * h + 2 * y + core for x in range(4) for y in range(4)]
        for z in range(4)
        for h in range(2)
        for core in range(2)
    ]
    return lax.all_to_all(value, BOTH, 0, 0, axis_index_groups=planes, tiled=True)


def sum_line(total):
    total = total.astype(BF16)
    came = [swap(total, d, 0).astype(F32) for d in (1, 2, 3)]
    total = ((total.astype(F32) + came[0]) + (came[1] + came[2])).astype(BF16)
    return total, swap(total, 3, 8)


def body(features_in, stencil, weights_first, weights_second, cotangent):
    height, breadth, channels = features_in.shape
    scale = 1.0 / math.sqrt(height * breadth * lax.axis_size("row") * lax.axis_size("col"))
    flat = stencil.reshape(21, height, breadth)
    stencil_t = jnp.pad(flat.transpose(1, 0, 2), ((0, 0), (0, SLOTS - 21), (0, 0)))
    w1 = weights_first.reshape(4 * channels, channels)
    w1t = weights_first.transpose(0, 2, 1).reshape(4 * channels, channels)
    w2t = weights_second.transpose(0, 2, 1).reshape(4 * channels, channels)

    rims = exchange(*pack(features_in, cotangent, flat), corner_kernel, "pack_corners")
    grad, *messages, keep, send = gradients(features_in, cotangent, stencil_t, rims, w1, w2t)
    row0, row1, col0, col1 = messages
    row0, row1 = pair_swap(row0, "row", 0), pair_swap(row1, "row", 1)
    half = (keep + swap(send, 0, 1)).astype(BF16)
    half, row0, row1 = lax.optimization_barrier((half, row0, row1))
    col0, col1 = add_corners(row0, row1, col0, col1, grad_corner_kernel, "pack_grad_corners")
    col0, col1 = pair_swap(col0, "col", 0), pair_swap(col1, "col", 1)
    part = plane_trade(half).astype(F32).sum(0)
    part, col0, col1 = lax.optimization_barrier((part, col0, col1))
    part, other = sum_line(part)
    part = (part.astype(F32) + other.astype(F32)).astype(BF16)
    part, grad = lax.optimization_barrier((part, grad))
    input_grad = input_gradient(grad, (row0, row1, col0, col1), stencil_t, rims, w1t)
    mine = plane_trade(jnp.broadcast_to(part[None], keep.shape))
    mine, input_grad = lax.optimization_barrier((mine, input_grad))
    theirs = swap(mine, 0, 1)
    mine, theirs = mine.astype(F32) * scale, theirs.astype(F32) * scale
    second = jnp.where(even("col"), mine, theirs).reshape(4, channels, channels)
    first = jnp.where(even("col"), theirs, mine).reshape(4, channels, channels)
    return input_grad, first, second


def solution(mesh):
    return jax.shard_map(
        body,
        mesh=mesh,
        in_specs=(
            P("row", "col", None),
            P(None, None, "row", "col"),
            P(),
            P(),
            P("row", "col", None),
        ),
        out_specs=(P("row", "col", None), P(), P()),
        check_vma=False,
    )
```

```python
import math

import jax
import jax.numpy as jnp
from jax import lax
from jax.experimental import pallas as pl
from jax.experimental.pallas import tpu as pltpu
from jax.sharding import PartitionSpec as P

F32 = jnp.float32
BF16 = jnp.bfloat16
BOTH = ("row", "col")
SLOTS = 32
LARGE = pltpu.CompilerParams(vmem_limit_bytes=24 * 1024 * 1024)
SMALL = pltpu.CompilerParams(vmem_limit_bytes=6 * 1024 * 1024)


def dot(lhs, rhs, lhs_dim, rhs_dim):
    return lax.dot_general(
        lhs, rhs, (((lhs_dim,), (rhs_dim,)), ((), ())), preferred_element_type=F32
    )


def iota(shape, dim):
    return lax.broadcasted_iota(jnp.int32, shape, dim)


def as_mask(condition):
    return jnp.where(condition, 1.0, 0.0).astype(BF16)


def halves(value):
    return jnp.concatenate([value[:, :128], value[:, 128:]], axis=0)


def whole(ref, start, rows):
    return jnp.concatenate([ref[start : start + rows], ref[start + rows : start + 2 * rows]], axis=1)


def even(axis):
    return lax.axis_index(axis) % 2 == 0


def choose(condition, value, other):
    return jnp.where(condition, value, other), jnp.where(condition, other, value)


def column_kernel(f_ref, c_ref, st_ref, col0_ref, col1_ref):
    breadth = f_ref.shape[1]
    sides = []
    for col, first in ((breadth - 1, (1, 5)), (0, (2, 6))):
        base = 0 if col == 0 else breadth - 16
        parts = []
        for ref in (f_ref, c_ref):
            parts.append(halves(ref[:, base : base + 16, :].astype(F32)[:, col - base, :]).astype(BF16))
        parts += [st_ref[7 * k + slot] for slot in first for k in range(3)]
        sides.append(parts)
    start = 0
    for right, left in zip(*sides):
        rows = right.shape[0]
        col0_ref[start : start + rows], col1_ref[start : start + rows] = choose(even("col"), right, left)
        start += rows


def pack_columns(features, cotangent, stencil):
    shape = jax.ShapeDtypeStruct((10 * features.shape[0], 128), BF16)
    return pl.pallas_call(
        column_kernel, out_shape=[shape] * 2, compiler_params=SMALL, name="pack_columns"
    )(features, cotangent, stencil)


def row_kernel(f_ref, c_ref, stt_ref, col0_ref, col1_ref, row0_ref, row1_ref):
    height = f_ref.shape[0]
    right, left = choose(even("col"), col0_ref[...].astype(F32), col1_ref[...].astype(F32))
    sides = []
    for row in (height - 2, 0):
        lines = []
        for r in (row, row + 1):
            for field in range(2):
                for rim in (left, right):
                    lines += [rim[(2 * field + h) * height + r :][:1] for h in range(2)]
        for r in (row, row + 1):
            for rim in (left, right):
                lines += [rim[(4 + n) * height + r :][:1] for n in range(6)]
        sides.append(jnp.concatenate(lines + [jnp.zeros((8, 128), F32)], axis=0).astype(BF16))
    for out, side, first in zip((row0_ref, row1_ref), choose(even("row"), *sides), (True, False)):
        base = jnp.where(even("row") == first, height - 2, 0)
        for field, ref in enumerate((f_ref, c_ref)):
            for r in range(2):
                start = 512 * field + 256 * r
                out[start : start + 256] = halves(ref[base + r])
        for r in range(2):
            out[1024 + SLOTS * r : 1024 + SLOTS * (r + 1)] = stt_ref[base + r]
        out[1088:1136] = side


def pack_rows(features, cotangent, stencil_t, cols):
    return pl.pallas_call(
        row_kernel,
        out_shape=[jax.ShapeDtypeStruct((1136, 128), BF16)] * 2,
        compiler_params=SMALL,
        name="pack_rows",
    )(features, cotangent, stencil_t, *cols)


def side_lines(rim, row, field, side):
    start = 1088 + 8 * row + 4 * field + 2 * side
    return jnp.concatenate([rim[start : start + 1], rim[start + 1 : start + 2]], axis=1)


def side_weights(rim, row, side, number):
    start = 1104 + 12 * row + 6 * side + number
    return rim[start : start + 1]


def pair_swap(value, axis, offset):
    rows, cols = lax.axis_size("row"), lax.axis_size("col")
    pairs = []
    for r in range(rows):
        for c in range(cols):
            place = r if axis == "row" else c
            step = 1 if place % 2 == offset else -1
            to_r, to_c = (r + step, c) if axis == "row" else (r, (c + step) % cols)
            if 0 <= to_r < rows:
                pairs.append((r * cols + c, to_r * cols + to_c))
    return lax.ppermute(value, BOTH, pairs)


def both_swaps(first, second, axis):
    return pair_swap(first, axis, 0), pair_swap(second, axis, 1)


def fill_masks(mask_ref):
    j, c = iota((128, 128), 0), iota((128, 128), 1)
    mask_ref[0] = as_mask(j == c)
    mask_ref[1] = as_mask(j == c + 1)
    mask_ref[2] = as_mask(j == c - 1)
    mask_ref[3] = as_mask(((j == 0) & (c < 2)) | ((j == 127) & ((c == 2) | (c == 3))))
    e, l = iota((16, 128), 0), iota((16, 128), 1)
    spots = ((0, 0), (1, 0), (2, 127), (3, 127))
    for number, (edge, lane) in enumerate(spots):
        mask_ref[4, 16 * number : 16 * number + 16] = as_mask((e == edge) & (l == lane))


def beside(left_near, left_far, right_near, right_far):
    lane = iota(left_near.shape, 1)
    spot = lambda value, shift, place: jnp.where(lane == place, pltpu.roll(value, shift, 1), 0.0)
    near = spot(left_near, 1, 0) + spot(right_near, 2, 2)
    return near, spot(left_far, 2, 1), spot(right_far, 3, 3)


def line(weights, slot):
    return jnp.broadcast_to(weights[slot : slot + 1], (16, 128)).astype(BF16)


def tall(value):
    return jnp.concatenate([value] * 8, axis=0)


def field_block(ext_ref, lx_ref, rx_ref, i):
    channels = ext_ref.shape[2]
    e = iota((16, channels), 0)
    edge = jnp.where(e == 0, lx_ref[pl.ds(i, 1)], 0.0)
    edge = jnp.where(e == 1, lx_ref[pl.ds(i - 1, 1)], edge)
    edge = jnp.where(e == 2, rx_ref[pl.ds(i, 1)], edge)
    edge = jnp.where(e == 3, rx_ref[pl.ds(i + 1, 1)], edge)
    rows = ext_ref[pl.ds(i - 1, 3)].reshape(384, channels)
    return jnp.concatenate([rows, edge.astype(BF16), jnp.zeros((112, channels), BF16)], axis=0)


def forward_band(wx_ref, mask_ref, i):
    weights = wx_ref[i].astype(F32)
    same, ahead, back = mask_ref[0], mask_ref[1], mask_ref[2]
    bands = []
    for k in range(3):
        w = [line(weights, 7 * k + s) for s in range(7)]
        t = [tall(x) for x in w]
        spots = [mask_ref[4, 16 * n : 16 * n + 16] for n in range(4)]
        edge = spots[0] * w[2] + spots[1] * w[6] + spots[2] * w[1] + spots[3] * w[5]
        bands.append(
            jnp.concatenate(
                [
                    same * t[4] + back * t[6],
                    same * t[0] + ahead * t[1] + back * t[2],
                    same * t[3] + ahead * t[5],
                    edge,
                    jnp.zeros((112, 128), BF16),
                ],
                axis=0,
            )
        )
    return jnp.concatenate(bands, axis=1)


def transposed_band(wx_ref, we_ref, mask_ref, i):
    before, here, after = (wx_ref[i + d].astype(F32) for d in (-1, 0, 1))
    same, ahead, back = mask_ref[0], mask_ref[1], mask_ref[2]
    bands = []
    for k in range(3):
        at = lambda weights, slot: tall(line(weights, 7 * k + slot))
        edge = we_ref[0, k, pl.ds(i, 1)] + we_ref[1, k, pl.ds(i - 1, 1)] + we_ref[2, k, pl.ds(i + 1, 1)]
        edge = jnp.broadcast_to(edge, (16, 128)).astype(BF16)
        bands.append(
            jnp.concatenate(
                [
                    same * at(before, 3) + ahead * at(before, 5),
                    same * at(here, 0) + ahead * at(here, 1) + back * at(here, 2),
                    same * at(after, 4) + back * at(after, 6),
                    mask_ref[3] * tall(edge),
                ],
                axis=1,
            )
        )
    return jnp.concatenate(bands, axis=0)


def spread(products):
    return [products[128 * k : 128 * k + 128].astype(BF16) for k in range(3)]


def stacks(f_ref, c_ref, wx_ref, we_ref, mask_ref, sides, i):
    flx_ref, frx_ref, clx_ref, crx_ref = sides
    forward = dot(forward_band(wx_ref, mask_ref, i), field_block(f_ref, flx_ref, frx_ref, i), 0, 0)
    turned = dot(
        transposed_band(wx_ref, we_ref, mask_ref, i), field_block(c_ref, clx_ref, crx_ref, i), 1, 0
    )
    return (
        jnp.concatenate([f_ref[i]] + spread(forward), axis=1),
        jnp.concatenate([c_ref[i]] + spread(turned), axis=1),
    )


def hidden_and_grad(ff, tt, w1, w2t):
    pre = dot(ff, w1, 1, 0)
    gate = jax.nn.sigmoid(pre)
    grad = dot(tt, w2t, 1, 0) * gate * (1.0 + pre * (1.0 - gate))
    return (pre * gate).astype(BF16), grad


def totals_of(hidden, tt, ff, grad):
    channels = hidden.shape[1]
    second = dot(hidden, tt, 0, 0)
    second = [
        second[:, k * channels : (k + 1) * channels].reshape(4, channels // 4, channels) for k in range(4)
    ]
    return second, dot(ff, grad, 0, 0).reshape(16, channels // 4, channels)


def inner_kernel(
    f_ref, c_ref, stt_ref, col0_ref, col1_ref, w1_ref, w2_ref,
    g_ref, total_ref, glx_ref, grx_ref,
    ff_ref, tt_ref, we_ref, mask_ref, *sides,
):
    height = f_ref.shape[0]
    fill_masks(mask_ref)
    right, left = choose(even("col"), col0_ref[...], col1_ref[...])
    for field in range(2):
        for rim, side in ((left, sides[2 * field]), (right, sides[2 * field + 1])):
            side[...] = whole(rim, 2 * field * height, height).astype(F32)
    for k in range(3):
        near, far = (4 + k) * height, (7 + k) * height
        weights = [rim[at : at + height].astype(F32) for rim in (left, right) for at in (near, far)]
        we_ref[0, k], we_ref[1, k], we_ref[2, k] = beside(*weights)

    @pl.loop(1, height - 1, unroll=7)
    def _(r):
        rows = pl.ds(pl.multiple_of((r - 1) * 128, 128), 128)
        ff_ref[rows], tt_ref[rows] = stacks(f_ref, c_ref, stt_ref, we_ref, mask_ref, sides, r)

    batch = (height - 2) // 2
    for i in range(2):
        rows = pl.ds(i * batch * 128, batch * 128)
        hidden, grad = hidden_and_grad(ff_ref[rows], tt_ref[rows], w1_ref[...], w2_ref[...])
        for q in range(batch):
            g_ref[i * batch + q] = grad[q * 128 : q * 128 + 128].astype(BF16)
            row = 1 + i * batch + q
            glx_ref[row : row + 1] = grad[q * 128 : q * 128 + 1]
            grx_ref[row : row + 1] = grad[q * 128 + 127 : q * 128 + 128]
        second, first = totals_of(hidden, tt_ref[rows], ff_ref[rows], grad.astype(BF16))
        for k in range(4):
            total_ref[0, 4 * k : 4 * k + 4] = second[k] if i == 0 else total_ref[0, 4 * k : 4 * k + 4] + second[k]
        total_ref[1] = first if i == 0 else total_ref[1] + first


def outer_kernel(
    f_ref, c_ref, stt_ref, col0_ref, col1_ref, row0_ref, row1_ref, w1_ref, w2_ref,
    total_ref, glx_ref, grx_ref,
    g_ref, gcol0_ref, gcol1_ref, keep_ref, send_ref,
    fext_ref, cext_ref, wx_ref, we_ref, mask_ref, *sides,
):
    height, breadth, channels = f_ref.shape
    fill_masks(mask_ref)
    below, above = choose(even("row"), row0_ref[...], row1_ref[...])
    right, left = choose(even("col"), col0_ref[...], col1_ref[...])
    ends = (0, 1, height - 2, height - 1)
    for n, (rim, at) in enumerate(((above, 0), (below, 6))):
        for r in range(2):
            fext_ref[at + r] = whole(rim, 256 * r, breadth)
            cext_ref[at + r] = whole(rim, 512 + 256 * r, breadth)
            wx_ref[at + r] = rim[1024 + SLOTS * r : 1024 + SLOTS * (r + 1)]
    for n, r in enumerate(ends):
        fext_ref[2 + n] = f_ref[r]
        cext_ref[2 + n] = c_ref[r]
        wx_ref[2 + n] = stt_ref[r]
    above, below = above.astype(F32), below.astype(F32)
    picked = lambda value: [value[r : r + 1] for r in ends]
    rims = (left.astype(F32), right.astype(F32))
    for field in range(2):
        for side in range(2):
            own = whole(rims[side], 2 * field * height, height)
            lines = [side_lines(above, r, field, side) for r in range(2)] + picked(own)
            lines += [side_lines(below, r, field, side) for r in range(2)]
            sides[2 * field + side][...] = jnp.concatenate(lines, axis=0)
    for k in range(3):
        weights = []
        for side in range(2):
            for number in (k, 3 + k):
                own = rims[side][(4 + number) * height : (5 + number) * height]
                lines = [side_weights(above, r, side, number) for r in range(2)] + picked(own)
                lines += [side_weights(below, r, side, number) for r in range(2)]
                weights.append(jnp.concatenate(lines, axis=0))
        we_ref[0, k], we_ref[1, k], we_ref[2, k] = beside(*weights)

    made = [stacks(fext_ref, cext_ref, wx_ref, we_ref, mask_ref, sides, i) for i in (2, 5, 1, 6)]
    ff = jnp.concatenate([m[0] for m in made], axis=0)
    tt = jnp.concatenate([m[1] for m in made], axis=0)
    hidden, grad = hidden_and_grad(ff, tt, w1_ref[...], w2_ref[...])
    own = 2 * breadth
    row, last = lax.axis_index("row"), lax.axis_size("row") - 1
    parts = [grad[128 * n : 128 * n + 128] for n in range(4)]
    parts[2] = jnp.where(row > 0, parts[2], 0.0)
    parts[3] = jnp.where(row < last, parts[3], 0.0)
    for n in range(4):
        g_ref[n] = parts[n].astype(BF16)
    spare = jnp.zeros((14, channels), F32)
    edges = []
    for inner, at in ((grx_ref, 127), (glx_ref, 0)):
        cut = lambda n: parts[n][at : at + 1]
        lines = [cut(2), cut(0), inner[1 : height - 1], cut(1), cut(3), spare]
        edges.append(jnp.concatenate(lines, axis=0).astype(BF16))
    gcol0_ref[...], gcol1_ref[...] = choose(even("col"), *edges)
    second, first = totals_of(hidden[:own], tt[:own], ff[:own], grad[:own].astype(BF16))
    core = lax.axis_index("col") % 2 == 0
    for k in range(4):
        at = slice(4 * k, 4 * k + 4)
        keep_ref[at], send_ref[at] = choose(
            core, total_ref[0, at] + second[k], total_ref[1, at] + first[at]
        )


def input_kernel(
    inner_ref, outer_ref, gcol0_ref, gcol1_ref, stt_ref, col0_ref, col1_ref, row0_ref, row1_ref, w1t_ref,
    out_ref,
    gext_ref, tt_ref, wx_ref, we_ref, mask_ref, lx_ref, rx_ref,
):
    height, breadth, _ = out_ref.shape
    fill_masks(mask_ref)
    below, above = choose(even("row"), row0_ref[1024:], row1_ref[1024:])
    right, left = choose(even("col"), col0_ref[4 * height :], col1_ref[4 * height :])
    wx_ref[0] = above[SLOTS : 2 * SLOTS]
    wx_ref[1 : 1 + height] = stt_ref[...]
    wx_ref[1 + height] = below[0:SLOTS]
    above, below = above.astype(F32), below.astype(F32)
    spare = jnp.zeros((6, 128), F32)
    for k in range(3):
        weights = []
        for side, rim in enumerate((left, right)):
            for number in (k, 3 + k):
                at = 80 + 6 * side + number
                lines = [above[at + 12 : at + 13], rim[number * height : (number + 1) * height].astype(F32)]
                weights.append(jnp.concatenate(lines + [below[at : at + 1], spare], axis=0))
        we_ref[0, k], we_ref[1, k], we_ref[2, k] = beside(*weights)
    gext_ref[0], gext_ref[1] = outer_ref[2], outer_ref[0]
    gext_ref[2:height] = inner_ref[...]
    gext_ref[height], gext_ref[height + 1] = outer_ref[1], outer_ref[3]
    right, left = choose(even("col"), gcol0_ref[...].astype(F32), gcol1_ref[...].astype(F32))
    lx_ref[...], rx_ref[...] = left, right

    @pl.loop(0, height, unroll=8)
    def _(r):
        rows = pl.ds(pl.multiple_of(r * 128, 128), 128)
        turned = dot(
            transposed_band(wx_ref, we_ref, mask_ref, r + 1), field_block(gext_ref, lx_ref, rx_ref, r + 1), 1, 0
        )
        tt_ref[rows] = jnp.concatenate([gext_ref[r + 1]] + spread(turned), axis=1)

    batch = 4

    @pl.loop(0, height // batch)
    def _(i):
        rows = pl.ds(pl.multiple_of(i * batch * 128, batch * 128), batch * 128)
        result = dot(tt_ref[rows], w1t_ref[...], 1, 0).astype(BF16)
        for q in range(batch):
            out_ref[i * batch + q] = result[q * 128 : q * 128 + 128]


MASKS = pltpu.VMEM((5, 128, 128), BF16)


def inner_gradients(features, cotangent, stencil_t, cols, w1, w2t):
    height, breadth, channels = features.shape
    shape = jax.ShapeDtypeStruct
    vertices = (height - 2) * breadth
    return pl.pallas_call(
        inner_kernel,
        out_shape=[
            shape((height - 2, breadth, channels), BF16),
            shape((2, 16, channels // 4, channels), F32),
            shape((height, channels), F32),
            shape((height, channels), F32),
        ],
        scratch_shapes=[
            pltpu.VMEM((vertices, 4 * channels), BF16),
            pltpu.VMEM((vertices, 4 * channels), BF16),
            pltpu.VMEM((3, 3, height, 128), F32),
            MASKS,
        ]
        + [pltpu.VMEM((height, channels), F32)] * 4,
        compiler_params=LARGE,
        cost_estimate=pl.CostEstimate(
            flops=9 * 10**9, bytes_accessed=9 * 10**6, transcendentals=vertices * channels
        ),
        name="inner_gradients",
    )(features, cotangent, stencil_t, *cols, w1, w2t)


def outer_gradients(features, cotangent, stencil_t, cols, rows, w1, w2t, inner):
    height, breadth, channels = features.shape
    shape = jax.ShapeDtypeStruct
    totals = (16, channels // 4, channels)
    return pl.pallas_call(
        outer_kernel,
        out_shape=[
            shape((4, breadth, channels), BF16),
            shape((height + 16, channels), BF16),
            shape((height + 16, channels), BF16),
            shape(totals, F32),
            shape(totals, F32),
        ],
        scratch_shapes=[
            pltpu.VMEM((8, breadth, channels), BF16),
            pltpu.VMEM((8, breadth, channels), BF16),
            pltpu.VMEM((8, SLOTS, 128), BF16),
            pltpu.VMEM((3, 3, 8, 128), F32),
            MASKS,
        ]
        + [pltpu.VMEM((8, channels), F32)] * 4,
        compiler_params=LARGE,
        cost_estimate=pl.CostEstimate(flops=2 * 10**9, bytes_accessed=5 * 10**6, transcendentals=10**5),
        name="outer_gradients",
    )(features, cotangent, stencil_t, *cols, *rows, w1, w2t, *inner)


def input_gradient(inner, outer, gcols, stencil_t, cols, rows, w1t):
    breadth, channels = inner.shape[1:]
    height = inner.shape[0] + 2
    return pl.pallas_call(
        input_kernel,
        out_shape=jax.ShapeDtypeStruct((height, breadth, channels), BF16),
        scratch_shapes=[
            pltpu.VMEM((height + 2, breadth, channels), BF16),
            pltpu.VMEM((height * breadth, 4 * channels), BF16),
            pltpu.VMEM((height + 2, SLOTS, 128), BF16),
            pltpu.VMEM((3, 3, height + 8, 128), F32),
            MASKS,
            pltpu.VMEM((height + 16, channels), F32),
            pltpu.VMEM((height + 16, channels), F32),
        ],
        compiler_params=LARGE,
        cost_estimate=pl.CostEstimate(flops=3 * 10**9, bytes_accessed=3 * 10**6, transcendentals=0),
        name="input_gradient",
    )(inner, outer, *gcols, stencil_t, *cols, *rows, w1t)


def swap(value, row_bits, col_bits):
    rows, cols = lax.axis_size("row"), lax.axis_size("col")
    pairs = [
        (r * cols + c, (r ^ row_bits) * cols + (c ^ col_bits)) for r in range(rows) for c in range(cols)
    ]
    return lax.ppermute(value, BOTH, pairs)


def plane_trade(value):
    cols = lax.axis_size("col")
    planes = [
        [cols * (4 * x + z) + 8 * h + 2 * y + core for x in range(4) for y in range(4)]
        for z in range(4)
        for h in range(2)
        for core in range(2)
    ]
    return lax.all_to_all(value, BOTH, 0, 0, axis_index_groups=planes, tiled=True)


def sum_line(total):
    total = total.astype(BF16)
    came = [swap(total, d, 0).astype(F32) for d in (1, 2, 3)]
    total = ((total.astype(F32) + came[0]) + (came[1] + came[2])).astype(BF16)
    return total, swap(total, 3, 8)


def body(features_in, stencil, weights_first, weights_second, cotangent):
    height, breadth, channels = features_in.shape
    scale = 1.0 / math.sqrt(height * breadth * lax.axis_size("row") * lax.axis_size("col"))
    flat = stencil.reshape(21, height, breadth)
    stencil_t = jnp.pad(flat.transpose(1, 0, 2), ((0, 0), (0, SLOTS - 21), (0, 0)))
    w1 = weights_first.reshape(4 * channels, channels)
    w1t = weights_first.transpose(0, 2, 1).reshape(4 * channels, channels)
    w2t = weights_second.transpose(0, 2, 1).reshape(4 * channels, channels)

    cols = both_swaps(*pack_columns(features_in, cotangent, flat), "col")
    rows = both_swaps(*pack_rows(features_in, cotangent, stencil_t, cols), "row")
    inner, *sums = inner_gradients(features_in, cotangent, stencil_t, cols, w1, w2t)
    outer, gcol0, gcol1, keep, send = outer_gradients(
        features_in, cotangent, stencil_t, cols, rows, w1, w2t, sums
    )
    half = (keep + swap(send, 0, 1)).astype(BF16)
    gcols = both_swaps(gcol0, gcol1, "col")
    part = plane_trade(half).astype(F32).sum(0)
    part, gcols = lax.optimization_barrier((part, gcols))
    part, other = sum_line(part)
    part = (part.astype(F32) + other.astype(F32)).astype(BF16)
    part, inner = lax.optimization_barrier((part, inner))
    input_grad = input_gradient(inner, outer, gcols, stencil_t, cols, rows, w1t)
    mine = plane_trade(jnp.broadcast_to(part[None], keep.shape))
    mine, input_grad = lax.optimization_barrier((mine, input_grad))
    theirs = swap(mine, 0, 1)
    mine, theirs = mine.astype(F32) * scale, theirs.astype(F32) * scale
    second = jnp.where(even("col"), mine, theirs).reshape(4, channels, channels)
    first = jnp.where(even("col"), theirs, mine).reshape(4, channels, channels)
    return input_grad, first, second


def solution(mesh):
    return jax.shard_map(
        body,
        mesh=mesh,
        in_specs=(
            P("row", "col", None),
            P(None, None, "row", "col"),
            P(),
            P(),
            P("row", "col", None),
        ),
        out_specs=(P("row", "col", None), P(), P()),
        check_vma=False,
    )
```

```python
import math

import jax
import jax.numpy as jnp
from jax import lax
from jax.experimental import pallas as pl
from jax.experimental.pallas import tpu as pltpu
from jax.sharding import PartitionSpec as P

F32 = jnp.float32
BF16 = jnp.bfloat16
BOTH = ("row", "col")
SLOTS = 32
LARGE = pltpu.CompilerParams(vmem_limit_bytes=24 * 1024 * 1024)
WIDE = pltpu.CompilerParams(vmem_limit_bytes=60 * 1024 * 1024)
SMALL = pltpu.CompilerParams(vmem_limit_bytes=6 * 1024 * 1024)


def dot(lhs, rhs, lhs_dim, rhs_dim):
    return lax.dot_general(
        lhs, rhs, (((lhs_dim,), (rhs_dim,)), ((), ())), preferred_element_type=F32
    )


def iota(shape, dim):
    return lax.broadcasted_iota(jnp.int32, shape, dim)


def as_mask(condition):
    return jnp.where(condition, 1.0, 0.0).astype(BF16)


def halves(value):
    return jnp.concatenate([value[:, :128], value[:, 128:]], axis=0)


def whole(ref, start, rows):
    return jnp.concatenate([ref[start : start + rows], ref[start + rows : start + 2 * rows]], axis=1)


def even(axis):
    return lax.axis_index(axis) % 2 == 0


def choose(condition, value, other):
    return jnp.where(condition, value, other), jnp.where(condition, other, value)


def column_kernel(f_ref, c_ref, stencil_ref, col0_ref, col1_ref, strip_ref, st_ref, sems):
    breadth = f_ref.shape[1]
    copies = [pltpu.make_async_copy(stencil_ref, st_ref, sems.at[4])]
    for n, base in enumerate((breadth - 16, 0)):
        for field, ref in enumerate((f_ref, c_ref)):
            at = 2 * n + field
            copies.append(pltpu.make_async_copy(ref.at[:, pl.ds(base, 16), :], strip_ref.at[at], sems.at[at]))
    for copy in copies:
        copy.start()
    for copy in copies:
        copy.wait()
    sides = []
    for n, (line_at, first) in enumerate(((15, (1, 5)), (0, (2, 6)))):
        parts = []
        for field in range(2):
            parts.append(halves(strip_ref[2 * n + field].astype(F32)[:, line_at, :]).astype(BF16))
        parts += [st_ref[7 * k + slot] for slot in first for k in range(3)]
        sides.append(parts)
    start = 0
    for right, left in zip(*sides):
        rows = right.shape[0]
        col0_ref[start : start + rows], col1_ref[start : start + rows] = choose(even("col"), right, left)
        start += rows


def pack_columns(features, cotangent, stencil):
    height, _, channels = features.shape
    shape = jax.ShapeDtypeStruct((10 * height, 128), BF16)
    return pl.pallas_call(
        column_kernel,
        out_shape=[shape] * 2,
        in_specs=[pl.BlockSpec(memory_space=pltpu.HBM)] * 3,
        scratch_shapes=[
            pltpu.VMEM((4, height, 16, channels), BF16),
            pltpu.VMEM(stencil.shape, BF16),
            pltpu.SemaphoreType.DMA((5,)),
        ],
        compiler_params=WIDE,
        name="pack_columns",
    )(features, cotangent, stencil)


def row_kernel(f_ref, c_ref, stt_ref, col0_ref, col1_ref, row0_ref, row1_ref):
    height = f_ref.shape[0]
    right, left = choose(even("col"), col0_ref[...].astype(F32), col1_ref[...].astype(F32))
    sides = []
    for row in (height - 2, 0):
        lines = []
        for r in (row, row + 1):
            for field in range(2):
                for rim in (left, right):
                    lines += [rim[(2 * field + h) * height + r :][:1] for h in range(2)]
        for r in (row, row + 1):
            for rim in (left, right):
                lines += [rim[(4 + n) * height + r :][:1] for n in range(6)]
        sides.append(jnp.concatenate(lines + [jnp.zeros((8, 128), F32)], axis=0).astype(BF16))
    for out, side, first in zip((row0_ref, row1_ref), choose(even("row"), *sides), (True, False)):
        base = jnp.where(even("row") == first, height - 2, 0)
        for field, ref in enumerate((f_ref, c_ref)):
            for r in range(2):
                start = 512 * field + 256 * r
                out[start : start + 256] = halves(ref[base + r])
        for r in range(2):
            out[1024 + SLOTS * r : 1024 + SLOTS * (r + 1)] = stt_ref[base + r]
        out[1088:1136] = side


def pack_rows(features, cotangent, stencil_t, cols):
    return pl.pallas_call(
        row_kernel,
        out_shape=[jax.ShapeDtypeStruct((1136, 128), BF16)] * 2,
        compiler_params=SMALL,
        name="pack_rows",
    )(features, cotangent, stencil_t, *cols)


def side_lines(rim, row, field, side):
    start = 1088 + 8 * row + 4 * field + 2 * side
    return jnp.concatenate([rim[start : start + 1], rim[start + 1 : start + 2]], axis=1)


def side_weights(rim, row, side, number):
    start = 1104 + 12 * row + 6 * side + number
    return rim[start : start + 1]


def pair_swap(value, axis, offset):
    rows, cols = lax.axis_size("row"), lax.axis_size("col")
    pairs = []
    for r in range(rows):
        for c in range(cols):
            place = r if axis == "row" else c
            step = 1 if place % 2 == offset else -1
            to_r, to_c = (r + step, c) if axis == "row" else (r, (c + step) % cols)
            if 0 <= to_r < rows:
                pairs.append((r * cols + c, to_r * cols + to_c))
    return lax.ppermute(value, BOTH, pairs)


def both_swaps(first, second, axis):
    return pair_swap(first, axis, 0), pair_swap(second, axis, 1)


def fill_masks(mask_ref):
    j, c = iota((128, 128), 0), iota((128, 128), 1)
    mask_ref[0] = as_mask(j == c)
    mask_ref[1] = as_mask(j == c + 1)
    mask_ref[2] = as_mask(j == c - 1)
    mask_ref[3] = as_mask(((j == 0) & (c < 2)) | ((j == 127) & ((c == 2) | (c == 3))))
    e, l = iota((16, 128), 0), iota((16, 128), 1)
    spots = ((0, 0), (1, 0), (2, 127), (3, 127))
    for number, (edge, lane) in enumerate(spots):
        mask_ref[4, 16 * number : 16 * number + 16] = as_mask((e == edge) & (l == lane))


def beside(left_near, left_far, right_near, right_far):
    lane = iota(left_near.shape, 1)
    spot = lambda value, shift, place: jnp.where(lane == place, pltpu.roll(value, shift, 1), 0.0)
    near = spot(left_near, 1, 0) + spot(right_near, 2, 2)
    return near, spot(left_far, 2, 1), spot(right_far, 3, 3)


def line(weights, slot):
    return jnp.broadcast_to(weights[slot : slot + 1], (16, 128)).astype(BF16)


def tall(value):
    return jnp.concatenate([value] * 8, axis=0)


def field_block(ext_ref, lx_ref, rx_ref, i):
    channels = ext_ref.shape[2]
    e = iota((16, channels), 0)
    edge = jnp.where(e == 0, lx_ref[pl.ds(i, 1)], 0.0)
    edge = jnp.where(e == 1, lx_ref[pl.ds(i - 1, 1)], edge)
    edge = jnp.where(e == 2, rx_ref[pl.ds(i, 1)], edge)
    edge = jnp.where(e == 3, rx_ref[pl.ds(i + 1, 1)], edge)
    rows = ext_ref[pl.ds(i - 1, 3)].reshape(384, channels)
    return jnp.concatenate([rows, edge.astype(BF16), jnp.zeros((112, channels), BF16)], axis=0)


def forward_band(wx_ref, mask_ref, i):
    weights = wx_ref[i].astype(F32)
    same, ahead, back = mask_ref[0], mask_ref[1], mask_ref[2]
    bands = []
    for k in range(3):
        w = [line(weights, 7 * k + s) for s in range(7)]
        t = [tall(x) for x in w]
        spots = [mask_ref[4, 16 * n : 16 * n + 16] for n in range(4)]
        edge = spots[0] * w[2] + spots[1] * w[6] + spots[2] * w[1] + spots[3] * w[5]
        bands.append(
            jnp.concatenate(
                [
                    same * t[4] + back * t[6],
                    same * t[0] + ahead * t[1] + back * t[2],
                    same * t[3] + ahead * t[5],
                    edge,
                    jnp.zeros((112, 128), BF16),
                ],
                axis=0,
            )
        )
    return jnp.concatenate(bands, axis=1)


def transposed_band(wx_ref, we_ref, mask_ref, i):
    before, here, after = (wx_ref[i + d].astype(F32) for d in (-1, 0, 1))
    same, ahead, back = mask_ref[0], mask_ref[1], mask_ref[2]
    bands = []
    for k in range(3):
        at = lambda weights, slot: tall(line(weights, 7 * k + slot))
        edge = we_ref[0, k, pl.ds(i, 1)] + we_ref[1, k, pl.ds(i - 1, 1)] + we_ref[2, k, pl.ds(i + 1, 1)]
        edge = jnp.broadcast_to(edge, (16, 128)).astype(BF16)
        bands.append(
            jnp.concatenate(
                [
                    same * at(before, 3) + ahead * at(before, 5),
                    same * at(here, 0) + ahead * at(here, 1) + back * at(here, 2),
                    same * at(after, 4) + back * at(after, 6),
                    mask_ref[3] * tall(edge),
                ],
                axis=1,
            )
        )
    return jnp.concatenate(bands, axis=0)


def spread(products):
    return [products[128 * k : 128 * k + 128].astype(BF16) for k in range(3)]


def stacks(f_ref, c_ref, wx_ref, we_ref, mask_ref, sides, i):
    flx_ref, frx_ref, clx_ref, crx_ref = sides
    forward = dot(forward_band(wx_ref, mask_ref, i), field_block(f_ref, flx_ref, frx_ref, i), 0, 0)
    turned = dot(
        transposed_band(wx_ref, we_ref, mask_ref, i), field_block(c_ref, clx_ref, crx_ref, i), 1, 0
    )
    return (
        jnp.concatenate([f_ref[i]] + spread(forward), axis=1),
        jnp.concatenate([c_ref[i]] + spread(turned), axis=1),
    )


def hidden_and_grad(ff, tt, w1, w2t):
    pre = dot(ff, w1, 1, 0)
    gate = jax.nn.sigmoid(pre)
    grad = dot(tt, w2t, 1, 0) * gate * (1.0 + pre * (1.0 - gate))
    return (pre * gate).astype(BF16), grad


def totals_of(hidden, tt, ff, grad):
    channels = hidden.shape[1]
    second = dot(hidden, tt, 0, 0)
    second = [
        second[:, k * channels : (k + 1) * channels].reshape(4, channels // 4, channels) for k in range(4)
    ]
    return second, dot(ff, grad, 0, 0).reshape(16, channels // 4, channels)


def inner_kernel(
    f_ref, c_ref, stt_ref, col0_ref, col1_ref, w1_ref, w2_ref,
    g_ref, total_ref, glx_ref, grx_ref,
    ff_ref, tt_ref, we_ref, mask_ref, *sides,
):
    height = f_ref.shape[0]
    fill_masks(mask_ref)
    right, left = choose(even("col"), col0_ref[...], col1_ref[...])
    for field in range(2):
        for rim, side in ((left, sides[2 * field]), (right, sides[2 * field + 1])):
            side[...] = whole(rim, 2 * field * height, height).astype(F32)
    for k in range(3):
        near, far = (4 + k) * height, (7 + k) * height
        weights = [rim[at : at + height].astype(F32) for rim in (left, right) for at in (near, far)]
        we_ref[0, k], we_ref[1, k], we_ref[2, k] = beside(*weights)

    @pl.loop(1, height - 1, unroll=7)
    def _(r):
        rows = pl.ds(pl.multiple_of((r - 1) * 128, 128), 128)
        ff_ref[rows], tt_ref[rows] = stacks(f_ref, c_ref, stt_ref, we_ref, mask_ref, sides, r)

    batch = (height - 2) // 2
    for i in range(2):
        rows = pl.ds(i * batch * 128, batch * 128)
        hidden, grad = hidden_and_grad(ff_ref[rows], tt_ref[rows], w1_ref[...], w2_ref[...])
        for q in range(batch):
            g_ref[i * batch + q] = grad[q * 128 : q * 128 + 128].astype(BF16)
            row = 1 + i * batch + q
            glx_ref[row : row + 1] = grad[q * 128 : q * 128 + 1]
            grx_ref[row : row + 1] = grad[q * 128 + 127 : q * 128 + 128]
        second, first = totals_of(hidden, tt_ref[rows], ff_ref[rows], grad.astype(BF16))
        for k in range(4):
            total_ref[0, 4 * k : 4 * k + 4] = second[k] if i == 0 else total_ref[0, 4 * k : 4 * k + 4] + second[k]
        total_ref[1] = first if i == 0 else total_ref[1] + first


def outer_kernel(
    f_ref, c_ref, stt_ref, col0_ref, col1_ref, row0_ref, row1_ref, w1_ref, w2_ref,
    total_ref, glx_ref, grx_ref,
    g_ref, gcol0_ref, gcol1_ref, keep_ref, send_ref,
    fext_ref, cext_ref, wx_ref, we_ref, mask_ref, *sides,
):
    height, breadth, channels = f_ref.shape
    fill_masks(mask_ref)
    below, above = choose(even("row"), row0_ref[...], row1_ref[...])
    right, left = choose(even("col"), col0_ref[...], col1_ref[...])
    ends = (0, 1, height - 2, height - 1)
    for n, (rim, at) in enumerate(((above, 0), (below, 6))):
        for r in range(2):
            fext_ref[at + r] = whole(rim, 256 * r, breadth)
            cext_ref[at + r] = whole(rim, 512 + 256 * r, breadth)
            wx_ref[at + r] = rim[1024 + SLOTS * r : 1024 + SLOTS * (r + 1)]
    for n, r in enumerate(ends):
        fext_ref[2 + n] = f_ref[r]
        cext_ref[2 + n] = c_ref[r]
        wx_ref[2 + n] = stt_ref[r]
    above, below = above.astype(F32), below.astype(F32)
    picked = lambda value: [value[r : r + 1] for r in ends]
    rims = (left.astype(F32), right.astype(F32))
    for field in range(2):
        for side in range(2):
            own = whole(rims[side], 2 * field * height, height)
            lines = [side_lines(above, r, field, side) for r in range(2)] + picked(own)
            lines += [side_lines(below, r, field, side) for r in range(2)]
            sides[2 * field + side][...] = jnp.concatenate(lines, axis=0)
    for k in range(3):
        weights = []
        for side in range(2):
            for number in (k, 3 + k):
                own = rims[side][(4 + number) * height : (5 + number) * height]
                lines = [side_weights(above, r, side, number) for r in range(2)] + picked(own)
                lines += [side_weights(below, r, side, number) for r in range(2)]
                weights.append(jnp.concatenate(lines, axis=0))
        we_ref[0, k], we_ref[1, k], we_ref[2, k] = beside(*weights)

    made = [stacks(fext_ref, cext_ref, wx_ref, we_ref, mask_ref, sides, i) for i in (2, 5, 1, 6)]
    ff = jnp.concatenate([m[0] for m in made], axis=0)
    tt = jnp.concatenate([m[1] for m in made], axis=0)
    hidden, grad = hidden_and_grad(ff, tt, w1_ref[...], w2_ref[...])
    own = 2 * breadth
    row, last = lax.axis_index("row"), lax.axis_size("row") - 1
    parts = [grad[128 * n : 128 * n + 128] for n in range(4)]
    parts[2] = jnp.where(row > 0, parts[2], 0.0)
    parts[3] = jnp.where(row < last, parts[3], 0.0)
    for n in range(4):
        g_ref[n] = parts[n].astype(BF16)
    spare = jnp.zeros((14, channels), F32)
    edges = []
    for inner, at in ((grx_ref, 127), (glx_ref, 0)):
        cut = lambda n: parts[n][at : at + 1]
        lines = [cut(2), cut(0), inner[1 : height - 1], cut(1), cut(3), spare]
        edges.append(jnp.concatenate(lines, axis=0).astype(BF16))
    gcol0_ref[...], gcol1_ref[...] = choose(even("col"), *edges)
    second, first = totals_of(hidden[:own], tt[:own], ff[:own], grad[:own].astype(BF16))
    core = lax.axis_index("col") % 2 == 0
    for k in range(4):
        at = slice(4 * k, 4 * k + 4)
        keep_ref[at], send = choose(core, total_ref[0, at] + second[k], total_ref[1, at] + first[at])
        send_ref[at] = send.astype(BF16)


def input_kernel(
    inner_ref, outer_ref, gcol0_ref, gcol1_ref, stt_ref, col0_ref, col1_ref, row0_ref, row1_ref, w1t_ref,
    out_ref,
    gext_ref, tt_ref, wx_ref, we_ref, mask_ref, lx_ref, rx_ref,
):
    height, breadth, _ = out_ref.shape
    fill_masks(mask_ref)
    below, above = choose(even("row"), row0_ref[1024:], row1_ref[1024:])
    right, left = choose(even("col"), col0_ref[4 * height :], col1_ref[4 * height :])
    wx_ref[0] = above[SLOTS : 2 * SLOTS]
    wx_ref[1 : 1 + height] = stt_ref[...]
    wx_ref[1 + height] = below[0:SLOTS]
    above, below = above.astype(F32), below.astype(F32)
    spare = jnp.zeros((6, 128), F32)
    for k in range(3):
        weights = []
        for side, rim in enumerate((left, right)):
            for number in (k, 3 + k):
                at = 80 + 6 * side + number
                lines = [above[at + 12 : at + 13], rim[number * height : (number + 1) * height].astype(F32)]
                weights.append(jnp.concatenate(lines + [below[at : at + 1], spare], axis=0))
        we_ref[0, k], we_ref[1, k], we_ref[2, k] = beside(*weights)
    gext_ref[0], gext_ref[1] = outer_ref[2], outer_ref[0]
    gext_ref[2:height] = inner_ref[...]
    gext_ref[height], gext_ref[height + 1] = outer_ref[1], outer_ref[3]
    right, left = choose(even("col"), gcol0_ref[...].astype(F32), gcol1_ref[...].astype(F32))
    lx_ref[...], rx_ref[...] = left, right

    @pl.loop(0, height, unroll=8)
    def _(r):
        rows = pl.ds(pl.multiple_of(r * 128, 128), 128)
        turned = dot(
            transposed_band(wx_ref, we_ref, mask_ref, r + 1), field_block(gext_ref, lx_ref, rx_ref, r + 1), 1, 0
        )
        tt_ref[rows] = jnp.concatenate([gext_ref[r + 1]] + spread(turned), axis=1)

    batch = 4

    @pl.loop(0, height // batch)
    def _(i):
        rows = pl.ds(pl.multiple_of(i * batch * 128, batch * 128), batch * 128)
        result = dot(tt_ref[rows], w1t_ref[...], 1, 0).astype(BF16)
        for q in range(batch):
            out_ref[i * batch + q] = result[q * 128 : q * 128 + 128]


MASKS = pltpu.VMEM((5, 128, 128), BF16)


def inner_gradients(features, cotangent, stencil_t, cols, w1, w2t):
    height, breadth, channels = features.shape
    shape = jax.ShapeDtypeStruct
    vertices = (height - 2) * breadth
    return pl.pallas_call(
        inner_kernel,
        out_shape=[
            shape((height - 2, breadth, channels), BF16),
            shape((2, 16, channels // 4, channels), F32),
            shape((height, channels), F32),
            shape((height, channels), F32),
        ],
        scratch_shapes=[
            pltpu.VMEM((vertices, 4 * channels), BF16),
            pltpu.VMEM((vertices, 4 * channels), BF16),
            pltpu.VMEM((3, 3, height, 128), F32),
            MASKS,
        ]
        + [pltpu.VMEM((height, channels), F32)] * 4,
        compiler_params=LARGE,
        cost_estimate=pl.CostEstimate(
            flops=9 * 10**9, bytes_accessed=9 * 10**6, transcendentals=vertices * channels
        ),
        name="inner_gradients",
    )(features, cotangent, stencil_t, *cols, w1, w2t)


def outer_gradients(features, cotangent, stencil_t, cols, rows, w1, w2t, inner):
    height, breadth, channels = features.shape
    shape = jax.ShapeDtypeStruct
    totals = (16, channels // 4, channels)
    return pl.pallas_call(
        outer_kernel,
        out_shape=[
            shape((4, breadth, channels), BF16),
            shape((height + 16, channels), BF16),
            shape((height + 16, channels), BF16),
            shape(totals, F32),
            shape(totals, BF16),
        ],
        scratch_shapes=[
            pltpu.VMEM((8, breadth, channels), BF16),
            pltpu.VMEM((8, breadth, channels), BF16),
            pltpu.VMEM((8, SLOTS, 128), BF16),
            pltpu.VMEM((3, 3, 8, 128), F32),
            MASKS,
        ]
        + [pltpu.VMEM((8, channels), F32)] * 4,
        compiler_params=LARGE,
        cost_estimate=pl.CostEstimate(flops=2 * 10**9, bytes_accessed=5 * 10**6, transcendentals=10**5),
        name="outer_gradients",
    )(features, cotangent, stencil_t, *cols, *rows, w1, w2t, *inner)


def input_gradient(inner, outer, gcols, stencil_t, cols, rows, w1t):
    breadth, channels = inner.shape[1:]
    height = inner.shape[0] + 2
    return pl.pallas_call(
        input_kernel,
        out_shape=jax.ShapeDtypeStruct((height, breadth, channels), BF16),
        scratch_shapes=[
            pltpu.VMEM((height + 2, breadth, channels), BF16),
            pltpu.VMEM((height * breadth, 4 * channels), BF16),
            pltpu.VMEM((height + 2, SLOTS, 128), BF16),
            pltpu.VMEM((3, 3, height + 8, 128), F32),
            MASKS,
            pltpu.VMEM((height + 16, channels), F32),
            pltpu.VMEM((height + 16, channels), F32),
        ],
        compiler_params=WIDE,
        cost_estimate=pl.CostEstimate(flops=3 * 10**9, bytes_accessed=3 * 10**6, transcendentals=0),
        name="input_gradient",
    )(inner, outer, *gcols, stencil_t, *cols, *rows, w1t)


def swap(value, row_bits, col_bits):
    rows, cols = lax.axis_size("row"), lax.axis_size("col")
    pairs = [
        (r * cols + c, (r ^ row_bits) * cols + (c ^ col_bits)) for r in range(rows) for c in range(cols)
    ]
    return lax.ppermute(value, BOTH, pairs)


def plane_trade(value):
    cols = lax.axis_size("col")
    planes = [
        [cols * (4 * x + z) + 8 * h + 2 * y + core for x in range(4) for y in range(4)]
        for z in range(4)
        for h in range(2)
        for core in range(2)
    ]
    return lax.all_to_all(value, BOTH, 0, 0, axis_index_groups=planes, tiled=True)


def sum_line(total):
    total = total.astype(BF16)
    came = [swap(total, d, 0).astype(F32) for d in (1, 2, 3)]
    total = ((total.astype(F32) + came[0]) + (came[1] + came[2])).astype(BF16)
    return total, swap(total, 3, 8)


def body(features_in, stencil, weights_first, weights_second, cotangent):
    height, breadth, channels = features_in.shape
    scale = 1.0 / math.sqrt(height * breadth * lax.axis_size("row") * lax.axis_size("col"))
    flat = stencil.reshape(21, height, breadth)
    stencil_t = jnp.pad(flat.transpose(1, 0, 2), ((0, 0), (0, SLOTS - 21), (0, 0)))
    w1 = weights_first.reshape(4 * channels, channels)
    w1t = weights_first.transpose(0, 2, 1).reshape(4 * channels, channels)
    w2t = weights_second.transpose(0, 2, 1).reshape(4 * channels, channels)

    w1t, w2t = lax.optimization_barrier((w1t, w2t))
    cols = both_swaps(*pack_columns(features_in, cotangent, flat), "col")
    rows = both_swaps(*pack_rows(features_in, cotangent, stencil_t, cols), "row")
    inner, *sums = inner_gradients(features_in, cotangent, stencil_t, cols, w1, w2t)
    outer, gcol0, gcol1, keep, send = outer_gradients(
        features_in, cotangent, stencil_t, cols, rows, w1, w2t, sums
    )
    half = (keep + swap(send, 0, 1).astype(F32)).astype(BF16)
    gcols = both_swaps(gcol0, gcol1, "col")
    part = plane_trade(half).astype(F32).sum(0)
    part, gcols = lax.optimization_barrier((part, gcols))
    part, other = sum_line(part)
    part = (part.astype(F32) + other.astype(F32)).astype(BF16)
    part, gcols = lax.optimization_barrier((part, gcols))
    input_grad = input_gradient(inner, outer, gcols, stencil_t, cols, rows, w1t)
    mine = plane_trade(jnp.broadcast_to(part[None], keep.shape))
    mine, input_grad = lax.optimization_barrier((mine, input_grad))
    theirs = swap(mine, 0, 1)
    mine, theirs = mine.astype(F32) * scale, theirs.astype(F32) * scale
    second = jnp.where(even("col"), mine, theirs).reshape(4, channels, channels)
    first = jnp.where(even("col"), theirs, mine).reshape(4, channels, channels)
    return input_grad, first, second


def solution(mesh):
    return jax.shard_map(
        body,
        mesh=mesh,
        in_specs=(
            P("row", "col", None),
            P(None, None, "row", "col"),
            P(),
            P(),
            P("row", "col", None),
        ),
        out_specs=(P("row", "col", None), P(), P()),
        check_vma=False,
    )
```

```python
import math

import jax
import jax.numpy as jnp
from jax import lax
from jax.experimental import pallas as pl
from jax.experimental.pallas import tpu as pltpu
from jax.sharding import PartitionSpec as P

F32 = jnp.float32
BF16 = jnp.bfloat16
BOTH = ("row", "col")
SLOTS = 32
LARGE = pltpu.CompilerParams(vmem_limit_bytes=24 * 1024 * 1024)
WIDE = pltpu.CompilerParams(vmem_limit_bytes=60 * 1024 * 1024)
SMALL = pltpu.CompilerParams(vmem_limit_bytes=6 * 1024 * 1024)


def dot(lhs, rhs, lhs_dim, rhs_dim):
    return lax.dot_general(
        lhs, rhs, (((lhs_dim,), (rhs_dim,)), ((), ())), preferred_element_type=F32
    )


def iota(shape, dim):
    return lax.broadcasted_iota(jnp.int32, shape, dim)


def as_mask(condition):
    return jnp.where(condition, 1.0, 0.0).astype(BF16)


def halves(value):
    return jnp.concatenate([value[:, :128], value[:, 128:]], axis=0)


def whole(ref, start, rows):
    return jnp.concatenate([ref[start : start + rows], ref[start + rows : start + 2 * rows]], axis=1)


def even(axis):
    return lax.axis_index(axis) % 2 == 0


def choose(condition, value, other):
    return jnp.where(condition, value, other), jnp.where(condition, other, value)


def column_kernel(f_ref, c_ref, stencil_ref, col0_ref, col1_ref, strip_ref, st_ref, sems):
    breadth = f_ref.shape[1]
    copies = [pltpu.make_async_copy(stencil_ref, st_ref, sems.at[4])]
    for n, base in enumerate((breadth - 16, 0)):
        for field, ref in enumerate((f_ref, c_ref)):
            at = 2 * n + field
            copies.append(pltpu.make_async_copy(ref.at[:, pl.ds(base, 16), :], strip_ref.at[at], sems.at[at]))
    for copy in copies:
        copy.start()
    for copy in copies:
        copy.wait()
    sides = []
    for n, (line_at, first) in enumerate(((15, (1, 5)), (0, (2, 6)))):
        parts = []
        for field in range(2):
            parts.append(halves(strip_ref[2 * n + field].astype(F32)[:, line_at, :]).astype(BF16))
        parts += [st_ref[7 * k + slot] for slot in first for k in range(3)]
        sides.append(parts)
    start = 0
    for right, left in zip(*sides):
        rows = right.shape[0]
        col0_ref[start : start + rows], col1_ref[start : start + rows] = choose(even("col"), right, left)
        start += rows


def pack_columns(features, cotangent, stencil):
    height, _, channels = features.shape
    shape = jax.ShapeDtypeStruct((10 * height, 128), BF16)
    return pl.pallas_call(
        column_kernel,
        out_shape=[shape] * 2,
        in_specs=[pl.BlockSpec(memory_space=pltpu.HBM)] * 3,
        scratch_shapes=[
            pltpu.VMEM((4, height, 16, channels), BF16),
            pltpu.VMEM(stencil.shape, BF16),
            pltpu.SemaphoreType.DMA((5,)),
        ],
        compiler_params=WIDE,
        name="pack_columns",
    )(features, cotangent, stencil)


def row_kernel(f_ref, c_ref, stt_ref, col0_ref, col1_ref, row0_ref, row1_ref):
    height = f_ref.shape[0]
    right, left = choose(even("col"), col0_ref[...].astype(F32), col1_ref[...].astype(F32))
    sides = []
    for row in (height - 2, 0):
        lines = []
        for r in (row, row + 1):
            for field in range(2):
                for rim in (left, right):
                    lines += [rim[(2 * field + h) * height + r :][:1] for h in range(2)]
        for r in (row, row + 1):
            for rim in (left, right):
                lines += [rim[(4 + n) * height + r :][:1] for n in range(6)]
        sides.append(jnp.concatenate(lines + [jnp.zeros((8, 128), F32)], axis=0).astype(BF16))
    for out, side, first in zip((row0_ref, row1_ref), choose(even("row"), *sides), (True, False)):
        base = jnp.where(even("row") == first, height - 2, 0)
        for field, ref in enumerate((f_ref, c_ref)):
            for r in range(2):
                start = 512 * field + 256 * r
                out[start : start + 256] = halves(ref[base + r])
        for r in range(2):
            out[1024 + SLOTS * r : 1024 + SLOTS * (r + 1)] = stt_ref[base + r]
        out[1088:1136] = side


def pack_rows(features, cotangent, stencil_t, cols):
    return pl.pallas_call(
        row_kernel,
        out_shape=[jax.ShapeDtypeStruct((1136, 128), BF16)] * 2,
        compiler_params=SMALL,
        name="pack_rows",
    )(features, cotangent, stencil_t, *cols)


def side_lines(rim, row, field, side):
    start = 1088 + 8 * row + 4 * field + 2 * side
    return jnp.concatenate([rim[start : start + 1], rim[start + 1 : start + 2]], axis=1)


def side_weights(rim, row, side, number):
    start = 1104 + 12 * row + 6 * side + number
    return rim[start : start + 1]


def pair_swap(value, axis, offset):
    rows, cols = lax.axis_size("row"), lax.axis_size("col")
    pairs = []
    for r in range(rows):
        for c in range(cols):
            place = r if axis == "row" else c
            step = 1 if place % 2 == offset else -1
            to_r, to_c = (r + step, c) if axis == "row" else (r, (c + step) % cols)
            if 0 <= to_r < rows:
                pairs.append((r * cols + c, to_r * cols + to_c))
    return lax.ppermute(value, BOTH, pairs)


def both_swaps(first, second, axis):
    return pair_swap(first, axis, 0), pair_swap(second, axis, 1)


def fill_masks(mask_ref):
    j, c = iota((128, 128), 0), iota((128, 128), 1)
    mask_ref[0] = as_mask(j == c)
    mask_ref[1] = as_mask(j == c + 1)
    mask_ref[2] = as_mask(j == c - 1)
    mask_ref[3] = as_mask(((j == 0) & (c < 2)) | ((j == 127) & ((c == 2) | (c == 3))))
    e, l = iota((16, 128), 0), iota((16, 128), 1)
    spots = ((0, 0), (1, 0), (2, 127), (3, 127))
    for number, (edge, lane) in enumerate(spots):
        mask_ref[4, 16 * number : 16 * number + 16] = as_mask((e == edge) & (l == lane))


def beside(left_near, left_far, right_near, right_far):
    lane = iota(left_near.shape, 1)
    spot = lambda value, shift, place: jnp.where(lane == place, pltpu.roll(value, shift, 1), 0.0)
    near = spot(left_near, 1, 0) + spot(right_near, 2, 2)
    return near, spot(left_far, 2, 1), spot(right_far, 3, 3)


def line(weights, slot):
    return jnp.broadcast_to(weights[slot : slot + 1], (16, 128)).astype(BF16)


def tall(value):
    return jnp.concatenate([value] * 8, axis=0)


def field_block(ext_ref, lx_ref, rx_ref, i):
    channels = ext_ref.shape[2]
    e = iota((16, channels), 0)
    edge = jnp.where(e == 0, lx_ref[pl.ds(i, 1)], 0.0)
    edge = jnp.where(e == 1, lx_ref[pl.ds(i - 1, 1)], edge)
    edge = jnp.where(e == 2, rx_ref[pl.ds(i, 1)], edge)
    edge = jnp.where(e == 3, rx_ref[pl.ds(i + 1, 1)], edge)
    rows = ext_ref[pl.ds(i - 1, 3)].reshape(384, channels)
    return jnp.concatenate([rows, edge.astype(BF16), jnp.zeros((112, channels), BF16)], axis=0)


def forward_band(wx_ref, mask_ref, i):
    weights = wx_ref[i].astype(F32)
    same, ahead, back = mask_ref[0], mask_ref[1], mask_ref[2]
    bands = []
    for k in range(3):
        w = [line(weights, 7 * k + s) for s in range(7)]
        t = [tall(x) for x in w]
        spots = [mask_ref[4, 16 * n : 16 * n + 16] for n in range(4)]
        edge = spots[0] * w[2] + spots[1] * w[6] + spots[2] * w[1] + spots[3] * w[5]
        bands.append(
            jnp.concatenate(
                [
                    same * t[4] + back * t[6],
                    same * t[0] + ahead * t[1] + back * t[2],
                    same * t[3] + ahead * t[5],
                    edge,
                    jnp.zeros((112, 128), BF16),
                ],
                axis=0,
            )
        )
    return jnp.concatenate(bands, axis=1)


def transposed_band(wx_ref, we_ref, mask_ref, i):
    before, here, after = (wx_ref[i + d].astype(F32) for d in (-1, 0, 1))
    same, ahead, back = mask_ref[0], mask_ref[1], mask_ref[2]
    bands = []
    for k in range(3):
        at = lambda weights, slot: tall(line(weights, 7 * k + slot))
        edge = we_ref[0, k, pl.ds(i, 1)] + we_ref[1, k, pl.ds(i - 1, 1)] + we_ref[2, k, pl.ds(i + 1, 1)]
        edge = jnp.broadcast_to(edge, (16, 128)).astype(BF16)
        bands.append(
            jnp.concatenate(
                [
                    same * at(before, 3) + ahead * at(before, 5),
                    same * at(here, 0) + ahead * at(here, 1) + back * at(here, 2),
                    same * at(after, 4) + back * at(after, 6),
                    mask_ref[3] * tall(edge),
                ],
                axis=1,
            )
        )
    return jnp.concatenate(bands, axis=0)


def spread(products):
    return [products[128 * k : 128 * k + 128].astype(BF16) for k in range(3)]


def stacks(f_ref, c_ref, wx_ref, we_ref, mask_ref, sides, i):
    flx_ref, frx_ref, clx_ref, crx_ref = sides
    forward = dot(forward_band(wx_ref, mask_ref, i), field_block(f_ref, flx_ref, frx_ref, i), 0, 0)
    turned = dot(
        transposed_band(wx_ref, we_ref, mask_ref, i), field_block(c_ref, clx_ref, crx_ref, i), 1, 0
    )
    return (
        jnp.concatenate([f_ref[i]] + spread(forward), axis=1),
        jnp.concatenate([c_ref[i]] + spread(turned), axis=1),
    )


def hidden_and_grad(ff, tt, w1, w2t):
    pre = dot(ff, w1, 1, 0)
    gate = jax.nn.sigmoid(pre)
    grad = dot(tt, w2t, 1, 0) * gate * (1.0 + pre * (1.0 - gate))
    return (pre * gate).astype(BF16), grad


def totals_of(hidden, tt, ff, grad):
    channels = hidden.shape[1]
    second = dot(hidden, tt, 0, 0)
    second = [
        second[:, k * channels : (k + 1) * channels].reshape(4, channels // 4, channels) for k in range(4)
    ]
    return second, dot(ff, grad, 0, 0).reshape(16, channels // 4, channels)


def inner_kernel(
    f_ref, c_ref, stt_ref, col0_ref, col1_ref, w1_ref, w2_ref,
    g_ref, total_ref, glx_ref, grx_ref,
    ff_ref, tt_ref, we_ref, mask_ref, *sides,
):
    height = f_ref.shape[0]
    fill_masks(mask_ref)
    right, left = choose(even("col"), col0_ref[...], col1_ref[...])
    for field in range(2):
        for rim, side in ((left, sides[2 * field]), (right, sides[2 * field + 1])):
            side[...] = whole(rim, 2 * field * height, height).astype(F32)
    for k in range(3):
        near, far = (4 + k) * height, (7 + k) * height
        weights = [rim[at : at + height].astype(F32) for rim in (left, right) for at in (near, far)]
        we_ref[0, k], we_ref[1, k], we_ref[2, k] = beside(*weights)

    @pl.loop(1, height - 1, unroll=7)
    def _(r):
        rows = pl.ds(pl.multiple_of((r - 1) * 128, 128), 128)
        ff_ref[rows], tt_ref[rows] = stacks(f_ref, c_ref, stt_ref, we_ref, mask_ref, sides, r)

    batch = (height - 2) // 2
    for i in range(2):
        rows = pl.ds(i * batch * 128, batch * 128)
        hidden, grad = hidden_and_grad(ff_ref[rows], tt_ref[rows], w1_ref[...], w2_ref[...])
        for q in range(batch):
            g_ref[i * batch + q] = grad[q * 128 : q * 128 + 128].astype(BF16)
            row = 1 + i * batch + q
            glx_ref[row : row + 1] = grad[q * 128 : q * 128 + 1]
            grx_ref[row : row + 1] = grad[q * 128 + 127 : q * 128 + 128]
        second, first = totals_of(hidden, tt_ref[rows], ff_ref[rows], grad.astype(BF16))
        for k in range(4):
            total_ref[0, 4 * k : 4 * k + 4] = second[k] if i == 0 else total_ref[0, 4 * k : 4 * k + 4] + second[k]
        total_ref[1] = first if i == 0 else total_ref[1] + first


def outer_kernel(
    f_ref, c_ref, stt_ref, col0_ref, col1_ref, row0_ref, row1_ref, w1_ref, w2_ref,
    total_ref, glx_ref, grx_ref,
    g_ref, gcol0_ref, gcol1_ref, keep_ref, send_ref,
    fext_ref, cext_ref, wx_ref, we_ref, mask_ref, *sides,
):
    height, breadth, channels = f_ref.shape
    fill_masks(mask_ref)
    below, above = choose(even("row"), row0_ref[...], row1_ref[...])
    right, left = choose(even("col"), col0_ref[...], col1_ref[...])
    ends = (0, 1, height - 2, height - 1)
    for n, (rim, at) in enumerate(((above, 0), (below, 6))):
        for r in range(2):
            fext_ref[at + r] = whole(rim, 256 * r, breadth)
            cext_ref[at + r] = whole(rim, 512 + 256 * r, breadth)
            wx_ref[at + r] = rim[1024 + SLOTS * r : 1024 + SLOTS * (r + 1)]
    for n, r in enumerate(ends):
        fext_ref[2 + n] = f_ref[r]
        cext_ref[2 + n] = c_ref[r]
        wx_ref[2 + n] = stt_ref[r]
    above, below = above.astype(F32), below.astype(F32)
    picked = lambda value: [value[r : r + 1] for r in ends]
    rims = (left.astype(F32), right.astype(F32))
    for field in range(2):
        for side in range(2):
            own = whole(rims[side], 2 * field * height, height)
            lines = [side_lines(above, r, field, side) for r in range(2)] + picked(own)
            lines += [side_lines(below, r, field, side) for r in range(2)]
            sides[2 * field + side][...] = jnp.concatenate(lines, axis=0)
    for k in range(3):
        weights = []
        for side in range(2):
            for number in (k, 3 + k):
                own = rims[side][(4 + number) * height : (5 + number) * height]
                lines = [side_weights(above, r, side, number) for r in range(2)] + picked(own)
                lines += [side_weights(below, r, side, number) for r in range(2)]
                weights.append(jnp.concatenate(lines, axis=0))
        we_ref[0, k], we_ref[1, k], we_ref[2, k] = beside(*weights)

    made = [stacks(fext_ref, cext_ref, wx_ref, we_ref, mask_ref, sides, i) for i in (2, 5, 1, 6)]
    ff = jnp.concatenate([m[0] for m in made], axis=0)
    tt = jnp.concatenate([m[1] for m in made], axis=0)
    hidden, grad = hidden_and_grad(ff, tt, w1_ref[...], w2_ref[...])
    own = 2 * breadth
    row, last = lax.axis_index("row"), lax.axis_size("row") - 1
    parts = [grad[128 * n : 128 * n + 128] for n in range(4)]
    parts[2] = jnp.where(row > 0, parts[2], 0.0)
    parts[3] = jnp.where(row < last, parts[3], 0.0)
    for n in range(4):
        g_ref[n] = parts[n].astype(BF16)
    spare = jnp.zeros((14, channels), F32)
    edges = []
    for inner, at in ((grx_ref, 127), (glx_ref, 0)):
        cut = lambda n: parts[n][at : at + 1]
        lines = [cut(2), cut(0), inner[1 : height - 1], cut(1), cut(3), spare]
        edges.append(jnp.concatenate(lines, axis=0).astype(BF16))
    gcol0_ref[...], gcol1_ref[...] = choose(even("col"), *edges)
    second, first = totals_of(hidden[:own], tt[:own], ff[:own], grad[:own].astype(BF16))
    core = lax.axis_index("col") % 2 == 0
    for k in range(4):
        at = slice(4 * k, 4 * k + 4)
        keep_ref[at], send = choose(core, total_ref[0, at] + second[k], total_ref[1, at] + first[at])
        send_ref[at] = send.astype(BF16)


def input_kernel(
    inner_ref, outer_ref, gcol0_ref, gcol1_ref, stt_ref, col0_ref, col1_ref, row0_ref, row1_ref, w1t_ref,
    out_ref,
    gext_ref, tt_ref, wx_ref, we_ref, mask_ref, lx_ref, rx_ref,
):
    height, breadth, _ = out_ref.shape
    fill_masks(mask_ref)
    below, above = choose(even("row"), row0_ref[1024:], row1_ref[1024:])
    right, left = choose(even("col"), col0_ref[4 * height :], col1_ref[4 * height :])
    wx_ref[0] = above[SLOTS : 2 * SLOTS]
    wx_ref[1 : 1 + height] = stt_ref[...]
    wx_ref[1 + height] = below[0:SLOTS]
    above, below = above.astype(F32), below.astype(F32)
    spare = jnp.zeros((6, 128), F32)
    for k in range(3):
        weights = []
        for side, rim in enumerate((left, right)):
            for number in (k, 3 + k):
                at = 80 + 6 * side + number
                lines = [above[at + 12 : at + 13], rim[number * height : (number + 1) * height].astype(F32)]
                weights.append(jnp.concatenate(lines + [below[at : at + 1], spare], axis=0))
        we_ref[0, k], we_ref[1, k], we_ref[2, k] = beside(*weights)
    gext_ref[0], gext_ref[1] = outer_ref[2], outer_ref[0]
    gext_ref[2:height] = inner_ref[...]
    gext_ref[height], gext_ref[height + 1] = outer_ref[1], outer_ref[3]
    right, left = choose(even("col"), gcol0_ref[...].astype(F32), gcol1_ref[...].astype(F32))
    lx_ref[...], rx_ref[...] = left, right

    @pl.loop(0, height, unroll=8)
    def _(r):
        rows = pl.ds(pl.multiple_of(r * 128, 128), 128)
        turned = dot(
            transposed_band(wx_ref, we_ref, mask_ref, r + 1), field_block(gext_ref, lx_ref, rx_ref, r + 1), 1, 0
        )
        tt_ref[rows] = jnp.concatenate([gext_ref[r + 1]] + spread(turned), axis=1)

    batch = 4

    @pl.loop(0, height // batch)
    def _(i):
        rows = pl.ds(pl.multiple_of(i * batch * 128, batch * 128), batch * 128)
        result = dot(tt_ref[rows], w1t_ref[...], 1, 0).astype(BF16)
        for q in range(batch):
            out_ref[i * batch + q] = result[q * 128 : q * 128 + 128]


MASKS = pltpu.VMEM((5, 128, 128), BF16)


def inner_gradients(features, cotangent, stencil_t, cols, w1, w2t):
    height, breadth, channels = features.shape
    shape = jax.ShapeDtypeStruct
    vertices = (height - 2) * breadth
    return pl.pallas_call(
        inner_kernel,
        out_shape=[
            shape((height - 2, breadth, channels), BF16),
            shape((2, 16, channels // 4, channels), F32),
            shape((height, channels), F32),
            shape((height, channels), F32),
        ],
        scratch_shapes=[
            pltpu.VMEM((vertices, 4 * channels), BF16),
            pltpu.VMEM((vertices, 4 * channels), BF16),
            pltpu.VMEM((3, 3, height, 128), F32),
            MASKS,
        ]
        + [pltpu.VMEM((height, channels), F32)] * 4,
        compiler_params=LARGE,
        cost_estimate=pl.CostEstimate(
            flops=9 * 10**9, bytes_accessed=9 * 10**6, transcendentals=vertices * channels
        ),
        name="inner_gradients",
    )(features, cotangent, stencil_t, *cols, w1, w2t)


def outer_gradients(features, cotangent, stencil_t, cols, rows, w1, w2t, inner):
    height, breadth, channels = features.shape
    shape = jax.ShapeDtypeStruct
    totals = (16, channels // 4, channels)
    return pl.pallas_call(
        outer_kernel,
        out_shape=[
            shape((4, breadth, channels), BF16),
            shape((height + 16, channels), BF16),
            shape((height + 16, channels), BF16),
            shape(totals, F32),
            shape(totals, BF16),
        ],
        scratch_shapes=[
            pltpu.VMEM((8, breadth, channels), BF16),
            pltpu.VMEM((8, breadth, channels), BF16),
            pltpu.VMEM((8, SLOTS, 128), BF16),
            pltpu.VMEM((3, 3, 8, 128), F32),
            MASKS,
        ]
        + [pltpu.VMEM((8, channels), F32)] * 4,
        compiler_params=LARGE,
        cost_estimate=pl.CostEstimate(flops=2 * 10**9, bytes_accessed=5 * 10**6, transcendentals=10**5),
        name="outer_gradients",
    )(features, cotangent, stencil_t, *cols, *rows, w1, w2t, *inner)


def input_gradient(inner, outer, gcols, stencil_t, cols, rows, w1t):
    breadth, channels = inner.shape[1:]
    height = inner.shape[0] + 2
    return pl.pallas_call(
        input_kernel,
        out_shape=jax.ShapeDtypeStruct((height, breadth, channels), BF16),
        scratch_shapes=[
            pltpu.VMEM((height + 2, breadth, channels), BF16),
            pltpu.VMEM((height * breadth, 4 * channels), BF16),
            pltpu.VMEM((height + 2, SLOTS, 128), BF16),
            pltpu.VMEM((3, 3, height + 8, 128), F32),
            MASKS,
            pltpu.VMEM((height + 16, channels), F32),
            pltpu.VMEM((height + 16, channels), F32),
        ],
        compiler_params=pltpu.CompilerParams(vmem_limit_bytes=36 * 1024 * 1024),
        cost_estimate=pl.CostEstimate(flops=3 * 10**9, bytes_accessed=3 * 10**6, transcendentals=0),
        name="input_gradient",
    )(inner, outer, *gcols, stencil_t, *cols, *rows, w1t)


def swap(value, row_bits, col_bits):
    rows, cols = lax.axis_size("row"), lax.axis_size("col")
    pairs = [
        (r * cols + c, (r ^ row_bits) * cols + (c ^ col_bits)) for r in range(rows) for c in range(cols)
    ]
    return lax.ppermute(value, BOTH, pairs)


def plane_trade(value):
    cols = lax.axis_size("col")
    planes = [
        [cols * (4 * x + z) + 8 * h + 2 * y + core for x in range(4) for y in range(4)]
        for z in range(4)
        for h in range(2)
        for core in range(2)
    ]
    return lax.all_to_all(value, BOTH, 0, 0, axis_index_groups=planes, tiled=True)


def sum_line(total):
    total = total.astype(BF16)
    came = [swap(total, d, 0).astype(F32) for d in (1, 2, 3)]
    total = ((total.astype(F32) + came[0]) + (came[1] + came[2])).astype(BF16)
    return total, swap(total, 3, 8)


def body(features_in, stencil, weights_first, weights_second, cotangent):
    height, breadth, channels = features_in.shape
    scale = 1.0 / math.sqrt(height * breadth * lax.axis_size("row") * lax.axis_size("col"))
    flat = stencil.reshape(21, height, breadth)
    stencil_t = jnp.pad(flat.transpose(1, 0, 2), ((0, 0), (0, SLOTS - 21), (0, 0)))
    w1 = weights_first.reshape(4 * channels, channels)
    w1t = weights_first.transpose(0, 2, 1).reshape(4 * channels, channels)
    w2t = weights_second.transpose(0, 2, 1).reshape(4 * channels, channels)

    w1t, w2t = lax.optimization_barrier((w1t, w2t))
    cols = both_swaps(*pack_columns(features_in, cotangent, flat), "col")
    rows = both_swaps(*pack_rows(features_in, cotangent, stencil_t, cols), "row")
    inner, *sums = inner_gradients(features_in, cotangent, stencil_t, cols, w1, w2t)
    outer, gcol0, gcol1, keep, send = outer_gradients(
        features_in, cotangent, stencil_t, cols, rows, w1, w2t, sums
    )
    half = (keep + swap(send, 0, 1).astype(F32)).astype(BF16)
    gcols = both_swaps(gcol0, gcol1, "col")
    part = plane_trade(half).astype(F32).sum(0)
    part, gcols = lax.optimization_barrier((part, gcols))
    part, other = sum_line(part)
    part = (part.astype(F32) + other.astype(F32)).astype(BF16)
    part, gcols = lax.optimization_barrier((part, gcols))
    input_grad = input_gradient(inner, outer, gcols, stencil_t, cols, rows, w1t)
    mine = plane_trade(jnp.broadcast_to(part[None], keep.shape))
    mine, input_grad = lax.optimization_barrier((mine, input_grad))
    theirs = swap(mine, 0, 1)
    mine, theirs = mine.astype(F32) * scale, theirs.astype(F32) * scale
    second = jnp.where(even("col"), mine, theirs).reshape(4, channels, channels)
    first = jnp.where(even("col"), theirs, mine).reshape(4, channels, channels)
    return input_grad, first, second


def solution(mesh):
    return jax.shard_map(
        body,
        mesh=mesh,
        in_specs=(
            P("row", "col", None),
            P(None, None, "row", "col"),
            P(),
            P(),
            P("row", "col", None),
        ),
        out_specs=(P("row", "col", None), P(), P()),
        check_vma=False,
    )
```

```python
import math

import jax
import jax.numpy as jnp
from jax import lax
from jax.experimental import pallas as pl
from jax.experimental.pallas import tpu as pltpu
from jax.sharding import PartitionSpec as P

F32 = jnp.float32
BF16 = jnp.bfloat16
BOTH = ("row", "col")
SLOTS = 32
LARGE = pltpu.CompilerParams(vmem_limit_bytes=24 * 1024 * 1024)
WIDE = pltpu.CompilerParams(vmem_limit_bytes=60 * 1024 * 1024)
SMALL = pltpu.CompilerParams(vmem_limit_bytes=6 * 1024 * 1024)


def dot(lhs, rhs, lhs_dim, rhs_dim):
    return lax.dot_general(
        lhs, rhs, (((lhs_dim,), (rhs_dim,)), ((), ())), preferred_element_type=F32
    )


def iota(shape, dim):
    return lax.broadcasted_iota(jnp.int32, shape, dim)


def as_mask(condition):
    return jnp.where(condition, 1.0, 0.0).astype(BF16)


def halves(value):
    return jnp.concatenate([value[:, :128], value[:, 128:]], axis=0)


def whole(ref, start, rows):
    return jnp.concatenate([ref[start : start + rows], ref[start + rows : start + 2 * rows]], axis=1)


def even(axis):
    return lax.axis_index(axis) % 2 == 0


def choose(condition, value, other):
    return jnp.where(condition, value, other), jnp.where(condition, other, value)


def column_kernel(f_ref, c_ref, stencil_ref, col0_ref, col1_ref, strip_ref, st_ref, sems):
    breadth = f_ref.shape[1]
    copies = [pltpu.make_async_copy(stencil_ref, st_ref, sems.at[4])]
    for n, base in enumerate((breadth - 16, 0)):
        for field, ref in enumerate((f_ref, c_ref)):
            at = 2 * n + field
            copies.append(pltpu.make_async_copy(ref.at[:, pl.ds(base, 16), :], strip_ref.at[at], sems.at[at]))
    for copy in copies:
        copy.start()
    for copy in copies:
        copy.wait()
    sides = []
    for n, (line_at, first) in enumerate(((15, (1, 5)), (0, (2, 6)))):
        parts = []
        for field in range(2):
            parts.append(halves(strip_ref[2 * n + field].astype(F32)[:, line_at, :]).astype(BF16))
        parts += [st_ref[7 * k + slot] for slot in first for k in range(3)]
        sides.append(parts)
    start = 0
    for right, left in zip(*sides):
        rows = right.shape[0]
        col0_ref[start : start + rows], col1_ref[start : start + rows] = choose(even("col"), right, left)
        start += rows


def pack_columns(features, cotangent, stencil):
    height, _, channels = features.shape
    shape = jax.ShapeDtypeStruct((10 * height, 128), BF16)
    return pl.pallas_call(
        column_kernel,
        out_shape=[shape] * 2,
        in_specs=[pl.BlockSpec(memory_space=pltpu.HBM)] * 3,
        scratch_shapes=[
            pltpu.VMEM((4, height, 16, channels), BF16),
            pltpu.VMEM(stencil.shape, BF16),
            pltpu.SemaphoreType.DMA((5,)),
        ],
        compiler_params=WIDE,
        name="pack_columns",
    )(features, cotangent, stencil)


def row_kernel(f_ref, c_ref, stt_ref, col0_ref, col1_ref, row0_ref, row1_ref):
    height = f_ref.shape[0]
    right, left = choose(even("col"), col0_ref[...].astype(F32), col1_ref[...].astype(F32))
    sides = []
    for row in (height - 2, 0):
        lines = []
        for r in (row, row + 1):
            for field in range(2):
                for rim in (left, right):
                    lines += [rim[(2 * field + h) * height + r :][:1] for h in range(2)]
        for r in (row, row + 1):
            for rim in (left, right):
                lines += [rim[(4 + n) * height + r :][:1] for n in range(6)]
        sides.append(jnp.concatenate(lines + [jnp.zeros((8, 128), F32)], axis=0).astype(BF16))
    for out, side, first in zip((row0_ref, row1_ref), choose(even("row"), *sides), (True, False)):
        base = jnp.where(even("row") == first, height - 2, 0)
        for field, ref in enumerate((f_ref, c_ref)):
            for r in range(2):
                start = 512 * field + 256 * r
                out[start : start + 256] = halves(ref[base + r])
        for r in range(2):
            out[1024 + SLOTS * r : 1024 + SLOTS * (r + 1)] = stt_ref[base + r]
        out[1088:1136] = side


def pack_rows(features, cotangent, stencil_t, cols):
    return pl.pallas_call(
        row_kernel,
        out_shape=[jax.ShapeDtypeStruct((1136, 128), BF16)] * 2,
        compiler_params=SMALL,
        name="pack_rows",
    )(features, cotangent, stencil_t, *cols)


def side_lines(rim, row, field, side):
    start = 1088 + 8 * row + 4 * field + 2 * side
    return jnp.concatenate([rim[start : start + 1], rim[start + 1 : start + 2]], axis=1)


def side_weights(rim, row, side, number):
    start = 1104 + 12 * row + 6 * side + number
    return rim[start : start + 1]


def pair_swap(value, axis, offset):
    rows, cols = lax.axis_size("row"), lax.axis_size("col")
    pairs = []
    for r in range(rows):
        for c in range(cols):
            place = r if axis == "row" else c
            step = 1 if place % 2 == offset else -1
            to_r, to_c = (r + step, c) if axis == "row" else (r, (c + step) % cols)
            if 0 <= to_r < rows:
                pairs.append((r * cols + c, to_r * cols + to_c))
    return lax.ppermute(value, BOTH, pairs)


def both_swaps(first, second, axis):
    return pair_swap(first, axis, 0), pair_swap(second, axis, 1)


def fill_masks(mask_ref):
    j, c = iota((128, 128), 0), iota((128, 128), 1)
    mask_ref[0] = as_mask(j == c)
    mask_ref[1] = as_mask(j == c + 1)
    mask_ref[2] = as_mask(j == c - 1)
    mask_ref[3] = as_mask(((j == 0) & (c < 2)) | ((j == 127) & ((c == 2) | (c == 3))))
    e, l = iota((16, 128), 0), iota((16, 128), 1)
    spots = ((0, 0), (1, 0), (2, 127), (3, 127))
    for number, (edge, lane) in enumerate(spots):
        mask_ref[4, 16 * number : 16 * number + 16] = as_mask((e == edge) & (l == lane))


def beside(left_near, left_far, right_near, right_far):
    lane = iota(left_near.shape, 1)
    spot = lambda value, shift, place: jnp.where(lane == place, pltpu.roll(value, shift, 1), 0.0)
    near = spot(left_near, 1, 0) + spot(right_near, 2, 2)
    return near, spot(left_far, 2, 1), spot(right_far, 3, 3)


def line(weights, slot):
    return jnp.broadcast_to(weights[slot : slot + 1], (16, 128)).astype(BF16)


def tall(value):
    return jnp.concatenate([value] * 8, axis=0)


def field_block(ext_ref, lx_ref, rx_ref, i):
    channels = ext_ref.shape[2]
    e = iota((16, channels), 0)
    edge = jnp.where(e == 0, lx_ref[pl.ds(i, 1)], 0.0)
    edge = jnp.where(e == 1, lx_ref[pl.ds(i - 1, 1)], edge)
    edge = jnp.where(e == 2, rx_ref[pl.ds(i, 1)], edge)
    edge = jnp.where(e == 3, rx_ref[pl.ds(i + 1, 1)], edge)
    rows = ext_ref[pl.ds(i - 1, 3)].reshape(384, channels)
    return jnp.concatenate([rows, edge.astype(BF16), jnp.zeros((112, channels), BF16)], axis=0)


def forward_band(wx_ref, mask_ref, i):
    weights = wx_ref[i].astype(F32)
    same, ahead, back = mask_ref[0], mask_ref[1], mask_ref[2]
    bands = []
    for k in range(3):
        w = [line(weights, 7 * k + s) for s in range(7)]
        t = [tall(x) for x in w]
        spots = [mask_ref[4, 16 * n : 16 * n + 16] for n in range(4)]
        edge = spots[0] * w[2] + spots[1] * w[6] + spots[2] * w[1] + spots[3] * w[5]
        bands.append(
            jnp.concatenate(
                [
                    same * t[4] + back * t[6],
                    same * t[0] + ahead * t[1] + back * t[2],
                    same * t[3] + ahead * t[5],
                    edge,
                    jnp.zeros((112, 128), BF16),
                ],
                axis=0,
            )
        )
    return jnp.concatenate(bands, axis=1)


def transposed_band(wx_ref, we_ref, mask_ref, i):
    before, here, after = (wx_ref[i + d].astype(F32) for d in (-1, 0, 1))
    same, ahead, back = mask_ref[0], mask_ref[1], mask_ref[2]
    bands = []
    for k in range(3):
        at = lambda weights, slot: tall(line(weights, 7 * k + slot))
        edge = we_ref[0, k, pl.ds(i, 1)] + we_ref[1, k, pl.ds(i - 1, 1)] + we_ref[2, k, pl.ds(i + 1, 1)]
        edge = jnp.broadcast_to(edge, (16, 128)).astype(BF16)
        bands.append(
            jnp.concatenate(
                [
                    same * at(before, 3) + ahead * at(before, 5),
                    same * at(here, 0) + ahead * at(here, 1) + back * at(here, 2),
                    same * at(after, 4) + back * at(after, 6),
                    mask_ref[3] * tall(edge),
                ],
                axis=1,
            )
        )
    return jnp.concatenate(bands, axis=0)


def spread(products):
    return [products[128 * k : 128 * k + 128].astype(BF16) for k in range(3)]


def stacks(f_ref, c_ref, wx_ref, we_ref, mask_ref, sides, i):
    flx_ref, frx_ref, clx_ref, crx_ref = sides
    forward = dot(forward_band(wx_ref, mask_ref, i), field_block(f_ref, flx_ref, frx_ref, i), 0, 0)
    turned = dot(
        transposed_band(wx_ref, we_ref, mask_ref, i), field_block(c_ref, clx_ref, crx_ref, i), 1, 0
    )
    return (
        jnp.concatenate([f_ref[i]] + spread(forward), axis=1),
        jnp.concatenate([c_ref[i]] + spread(turned), axis=1),
    )


def hidden_and_grad(ff, tt, w1, w2t):
    pre = dot(ff, w1, 1, 0)
    gate = jax.nn.sigmoid(pre)
    grad = dot(tt, w2t, 1, 0) * gate * (1.0 + pre * (1.0 - gate))
    return (pre * gate).astype(BF16), grad


def totals_of(hidden, tt, ff, grad):
    channels = hidden.shape[1]
    second = dot(hidden, tt, 0, 0)
    second = [
        second[:, k * channels : (k + 1) * channels].reshape(4, channels // 4, channels) for k in range(4)
    ]
    return second, dot(ff, grad, 0, 0).reshape(16, channels // 4, channels)


def inner_kernel(
    f_ref, c_ref, stt_ref, col0_ref, col1_ref, w1_ref, w2_ref,
    g_ref, total_ref, glx_ref, grx_ref,
    ff_ref, tt_ref, we_ref, mask_ref, *sides,
):
    height = f_ref.shape[0]
    fill_masks(mask_ref)
    right, left = choose(even("col"), col0_ref[...], col1_ref[...])
    for field in range(2):
        for rim, side in ((left, sides[2 * field]), (right, sides[2 * field + 1])):
            side[...] = whole(rim, 2 * field * height, height).astype(F32)
    for k in range(3):
        near, far = (4 + k) * height, (7 + k) * height
        weights = [rim[at : at + height].astype(F32) for rim in (left, right) for at in (near, far)]
        we_ref[0, k], we_ref[1, k], we_ref[2, k] = beside(*weights)

    @pl.loop(1, height - 1, unroll=14)
    def _(r):
        rows = pl.ds(pl.multiple_of((r - 1) * 128, 128), 128)
        ff_ref[rows], tt_ref[rows] = stacks(f_ref, c_ref, stt_ref, we_ref, mask_ref, sides, r)

    batch = (height - 2) // 2
    for i in range(2):
        rows = pl.ds(i * batch * 128, batch * 128)
        hidden, grad = hidden_and_grad(ff_ref[rows], tt_ref[rows], w1_ref[...], w2_ref[...])
        for q in range(batch):
            g_ref[i * batch + q] = grad[q * 128 : q * 128 + 128].astype(BF16)
            row = 1 + i * batch + q
            glx_ref[row : row + 1] = grad[q * 128 : q * 128 + 1]
            grx_ref[row : row + 1] = grad[q * 128 + 127 : q * 128 + 128]
        second, first = totals_of(hidden, tt_ref[rows], ff_ref[rows], grad.astype(BF16))
        for k in range(4):
            total_ref[0, 4 * k : 4 * k + 4] = second[k] if i == 0 else total_ref[0, 4 * k : 4 * k + 4] + second[k]
        total_ref[1] = first if i == 0 else total_ref[1] + first


def outer_kernel(
    f_ref, c_ref, stt_ref, col0_ref, col1_ref, row0_ref, row1_ref, w1_ref, w2_ref,
    total_ref, glx_ref, grx_ref,
    g_ref, gcol0_ref, gcol1_ref, keep_ref, send_ref,
    fext_ref, cext_ref, wx_ref, we_ref, mask_ref, *sides,
):
    height, breadth, channels = f_ref.shape
    fill_masks(mask_ref)
    below, above = choose(even("row"), row0_ref[...], row1_ref[...])
    right, left = choose(even("col"), col0_ref[...], col1_ref[...])
    ends = (0, 1, height - 2, height - 1)
    for n, (rim, at) in enumerate(((above, 0), (below, 6))):
        for r in range(2):
            fext_ref[at + r] = whole(rim, 256 * r, breadth)
            cext_ref[at + r] = whole(rim, 512 + 256 * r, breadth)
            wx_ref[at + r] = rim[1024 + SLOTS * r : 1024 + SLOTS * (r + 1)]
    for n, r in enumerate(ends):
        fext_ref[2 + n] = f_ref[r]
        cext_ref[2 + n] = c_ref[r]
        wx_ref[2 + n] = stt_ref[r]
    above, below = above.astype(F32), below.astype(F32)
    picked = lambda value: [value[r : r + 1] for r in ends]
    rims = (left.astype(F32), right.astype(F32))
    for field in range(2):
        for side in range(2):
            own = whole(rims[side], 2 * field * height, height)
            lines = [side_lines(above, r, field, side) for r in range(2)] + picked(own)
            lines += [side_lines(below, r, field, side) for r in range(2)]
            sides[2 * field + side][...] = jnp.concatenate(lines, axis=0)
    for k in range(3):
        weights = []
        for side in range(2):
            for number in (k, 3 + k):
                own = rims[side][(4 + number) * height : (5 + number) * height]
                lines = [side_weights(above, r, side, number) for r in range(2)] + picked(own)
                lines += [side_weights(below, r, side, number) for r in range(2)]
                weights.append(jnp.concatenate(lines, axis=0))
        we_ref[0, k], we_ref[1, k], we_ref[2, k] = beside(*weights)

    made = [stacks(fext_ref, cext_ref, wx_ref, we_ref, mask_ref, sides, i) for i in (2, 5, 1, 6)]
    ff = jnp.concatenate([m[0] for m in made], axis=0)
    tt = jnp.concatenate([m[1] for m in made], axis=0)
    hidden, grad = hidden_and_grad(ff, tt, w1_ref[...], w2_ref[...])
    own = 2 * breadth
    row, last = lax.axis_index("row"), lax.axis_size("row") - 1
    parts = [grad[128 * n : 128 * n + 128] for n in range(4)]
    parts[2] = jnp.where(row > 0, parts[2], 0.0)
    parts[3] = jnp.where(row < last, parts[3], 0.0)
    for n in range(4):
        g_ref[n] = parts[n].astype(BF16)
    spare = jnp.zeros((14, channels), F32)
    edges = []
    for inner, at in ((grx_ref, 127), (glx_ref, 0)):
        cut = lambda n: parts[n][at : at + 1]
        lines = [cut(2), cut(0), inner[1 : height - 1], cut(1), cut(3), spare]
        edges.append(jnp.concatenate(lines, axis=0).astype(BF16))
    gcol0_ref[...], gcol1_ref[...] = choose(even("col"), *edges)
    second, first = totals_of(hidden[:own], tt[:own], ff[:own], grad[:own].astype(BF16))
    core = lax.axis_index("col") % 2 == 0
    for k in range(4):
        at = slice(4 * k, 4 * k + 4)
        keep_ref[at], send = choose(core, total_ref[0, at] + second[k], total_ref[1, at] + first[at])
        send_ref[at] = send.astype(BF16)


def input_kernel(
    inner_ref, outer_ref, gcol0_ref, gcol1_ref, stt_ref, col0_ref, col1_ref, row0_ref, row1_ref, w1t_ref,
    out_ref,
    gext_ref, tt_ref, wx_ref, we_ref, mask_ref, lx_ref, rx_ref,
):
    height, breadth, _ = out_ref.shape
    fill_masks(mask_ref)
    below, above = choose(even("row"), row0_ref[1024:], row1_ref[1024:])
    right, left = choose(even("col"), col0_ref[4 * height :], col1_ref[4 * height :])
    wx_ref[0] = above[SLOTS : 2 * SLOTS]
    wx_ref[1 : 1 + height] = stt_ref[...]
    wx_ref[1 + height] = below[0:SLOTS]
    above, below = above.astype(F32), below.astype(F32)
    spare = jnp.zeros((6, 128), F32)
    for k in range(3):
        weights = []
        for side, rim in enumerate((left, right)):
            for number in (k, 3 + k):
                at = 80 + 6 * side + number
                lines = [above[at + 12 : at + 13], rim[number * height : (number + 1) * height].astype(F32)]
                weights.append(jnp.concatenate(lines + [below[at : at + 1], spare], axis=0))
        we_ref[0, k], we_ref[1, k], we_ref[2, k] = beside(*weights)
    gext_ref[0], gext_ref[1] = outer_ref[2], outer_ref[0]
    gext_ref[2:height] = inner_ref[...]
    gext_ref[height], gext_ref[height + 1] = outer_ref[1], outer_ref[3]
    right, left = choose(even("col"), gcol0_ref[...].astype(F32), gcol1_ref[...].astype(F32))
    lx_ref[...], rx_ref[...] = left, right

    @pl.loop(0, height, unroll=8)
    def _(r):
        rows = pl.ds(pl.multiple_of(r * 128, 128), 128)
        turned = dot(
            transposed_band(wx_ref, we_ref, mask_ref, r + 1), field_block(gext_ref, lx_ref, rx_ref, r + 1), 1, 0
        )
        tt_ref[rows] = jnp.concatenate([gext_ref[r + 1]] + spread(turned), axis=1)

    batch = 4

    @pl.loop(0, height // batch)
    def _(i):
        rows = pl.ds(pl.multiple_of(i * batch * 128, batch * 128), batch * 128)
        result = dot(tt_ref[rows], w1t_ref[...], 1, 0).astype(BF16)
        for q in range(batch):
            out_ref[i * batch + q] = result[q * 128 : q * 128 + 128]


MASKS = pltpu.VMEM((5, 128, 128), BF16)


def inner_gradients(features, cotangent, stencil_t, cols, w1, w2t):
    height, breadth, channels = features.shape
    shape = jax.ShapeDtypeStruct
    vertices = (height - 2) * breadth
    return pl.pallas_call(
        inner_kernel,
        out_shape=[
            shape((height - 2, breadth, channels), BF16),
            shape((2, 16, channels // 4, channels), F32),
            shape((height, channels), F32),
            shape((height, channels), F32),
        ],
        scratch_shapes=[
            pltpu.VMEM((vertices, 4 * channels), BF16),
            pltpu.VMEM((vertices, 4 * channels), BF16),
            pltpu.VMEM((3, 3, height, 128), F32),
            MASKS,
        ]
        + [pltpu.VMEM((height, channels), F32)] * 4,
        compiler_params=LARGE,
        cost_estimate=pl.CostEstimate(
            flops=9 * 10**9, bytes_accessed=9 * 10**6, transcendentals=vertices * channels
        ),
        name="inner_gradients",
    )(features, cotangent, stencil_t, *cols, w1, w2t)


def outer_gradients(features, cotangent, stencil_t, cols, rows, w1, w2t, inner):
    height, breadth, channels = features.shape
    shape = jax.ShapeDtypeStruct
    totals = (16, channels // 4, channels)
    return pl.pallas_call(
        outer_kernel,
        out_shape=[
            shape((4, breadth, channels), BF16),
            shape((height + 16, channels), BF16),
            shape((height + 16, channels), BF16),
            shape(totals, F32),
            shape(totals, BF16),
        ],
        scratch_shapes=[
            pltpu.VMEM((8, breadth, channels), BF16),
            pltpu.VMEM((8, breadth, channels), BF16),
            pltpu.VMEM((8, SLOTS, 128), BF16),
            pltpu.VMEM((3, 3, 8, 128), F32),
            MASKS,
        ]
        + [pltpu.VMEM((8, channels), F32)] * 4,
        compiler_params=LARGE,
        cost_estimate=pl.CostEstimate(flops=2 * 10**9, bytes_accessed=5 * 10**6, transcendentals=10**5),
        name="outer_gradients",
    )(features, cotangent, stencil_t, *cols, *rows, w1, w2t, *inner)


def input_gradient(inner, outer, gcols, stencil_t, cols, rows, w1t):
    breadth, channels = inner.shape[1:]
    height = inner.shape[0] + 2
    return pl.pallas_call(
        input_kernel,
        out_shape=jax.ShapeDtypeStruct((height, breadth, channels), BF16),
        scratch_shapes=[
            pltpu.VMEM((height + 2, breadth, channels), BF16),
            pltpu.VMEM((height * breadth, 4 * channels), BF16),
            pltpu.VMEM((height + 2, SLOTS, 128), BF16),
            pltpu.VMEM((3, 3, height + 8, 128), F32),
            MASKS,
            pltpu.VMEM((height + 16, channels), F32),
            pltpu.VMEM((height + 16, channels), F32),
        ],
        compiler_params=pltpu.CompilerParams(vmem_limit_bytes=36 * 1024 * 1024),
        cost_estimate=pl.CostEstimate(flops=3 * 10**9, bytes_accessed=3 * 10**6, transcendentals=0),
        name="input_gradient",
    )(inner, outer, *gcols, stencil_t, *cols, *rows, w1t)


def swap(value, row_bits, col_bits):
    rows, cols = lax.axis_size("row"), lax.axis_size("col")
    pairs = [
        (r * cols + c, (r ^ row_bits) * cols + (c ^ col_bits)) for r in range(rows) for c in range(cols)
    ]
    return lax.ppermute(value, BOTH, pairs)


def plane_trade(value):
    cols = lax.axis_size("col")
    planes = [
        [cols * (4 * x + z) + 8 * h + 2 * y + core for x in range(4) for y in range(4)]
        for z in range(4)
        for h in range(2)
        for core in range(2)
    ]
    return lax.all_to_all(value, BOTH, 0, 0, axis_index_groups=planes, tiled=True)


def sum_line(total):
    total = total.astype(BF16)
    came = [swap(total, d, 0).astype(F32) for d in (1, 2, 3)]
    total = ((total.astype(F32) + came[0]) + (came[1] + came[2])).astype(BF16)
    return total, swap(total, 3, 8)


def copies_kernel(part_ref, other_ref, out_ref):
    total = (part_ref[...].astype(F32) + other_ref[...].astype(F32)).astype(BF16)
    for n in range(out_ref.shape[0]):
        out_ref[n] = total


def sum_copies(part, other, shape):
    return pl.pallas_call(
        copies_kernel, out_shape=jax.ShapeDtypeStruct(shape, BF16), compiler_params=SMALL, name="sum_copies"
    )(part, other)


def body(features_in, stencil, weights_first, weights_second, cotangent):
    height, breadth, channels = features_in.shape
    scale = 1.0 / math.sqrt(height * breadth * lax.axis_size("row") * lax.axis_size("col"))
    flat = stencil.reshape(21, height, breadth)
    stencil_t = jnp.pad(flat.transpose(1, 0, 2), ((0, 0), (0, SLOTS - 21), (0, 0)))
    w1 = weights_first.reshape(4 * channels, channels)
    w1t = weights_first.transpose(0, 2, 1).reshape(4 * channels, channels)
    w2t = weights_second.transpose(0, 2, 1).reshape(4 * channels, channels)

    w1t, w2t = lax.optimization_barrier((w1t, w2t))
    cols = both_swaps(*pack_columns(features_in, cotangent, flat), "col")
    rows = both_swaps(*pack_rows(features_in, cotangent, stencil_t, cols), "row")
    inner, *sums = inner_gradients(features_in, cotangent, stencil_t, cols, w1, w2t)
    outer, gcol0, gcol1, keep, send = outer_gradients(
        features_in, cotangent, stencil_t, cols, rows, w1, w2t, sums
    )
    half = (keep + swap(send, 0, 1).astype(F32)).astype(BF16)
    gcols = both_swaps(gcol0, gcol1, "col")
    part = plane_trade(half).astype(F32).sum(0)
    part, gcols = lax.optimization_barrier((part, gcols))
    part, other = sum_line(part)
    part, other, gcols = lax.optimization_barrier((part, other, gcols))
    input_grad = input_gradient(inner, outer, gcols, stencil_t, cols, rows, w1t)
    mine = plane_trade(sum_copies(part, other, keep.shape))
    mine, input_grad = lax.optimization_barrier((mine, input_grad))
    theirs = swap(mine, 0, 1)
    mine, theirs = mine.astype(F32) * scale, theirs.astype(F32) * scale
    second = jnp.where(even("col"), mine, theirs).reshape(4, channels, channels)
    first = jnp.where(even("col"), theirs, mine).reshape(4, channels, channels)
    return input_grad, first, second


def solution(mesh):
    return jax.shard_map(
        body,
        mesh=mesh,
        in_specs=(
            P("row", "col", None),
            P(None, None, "row", "col"),
            P(),
            P(),
            P("row", "col", None),
        ),
        out_specs=(P("row", "col", None), P(), P()),
        check_vma=False,
    )
```
